1024 devices in a mesh: gx: 64 (over x, z), gy: 16 (over y, core).
Axes of the slice: x: 8, y: 8, z: 8, core: 2. Of those that a mesh axis runs over, the one named last changes fastest.
Arguments:
- state: float32 [5, 192, 256, 128], P(None, 'gx', 'gy'), may hold values from -2 to 6, as said below
- lf_speed: float32 [3], replicated, may hold values from 2.5 to 4
- ghost_cell: int32 [64, 16, 16, 192], P('gx', 'gy'), may hold values from -1 to 6143, as said below
- ghost_frac: float32 [3, 64, 16, 16, 192], P(None, 'gx', 'gy'), may hold values from 0 to 1
- donor_block: int32 [64, 16, 16, 192], P('gx', 'gy'), may hold values from 0 to 3966, as said below
Outputs:
- advanced: float32 [5, 192, 256, 128], P(None, 'gx', 'gy')
The draws below stay inside these ranges and needn't reach their ends.
Inputs may be any that keep to these rules, and one draw needn't show every extreme that they name: `state`: state of an ideal gas with ratio of specific heats 1.4: density and pressure lie between 0.49 and 2.02 in every cell. `ghost_cell`: -1 marks an empty slot, and in each list [x, p, q, :] the live slots come first. A live slot holds (i * 16 + j) * 128 + k for a cell of brick (x, p); no cell appears twice among the lists of a brick. In every draw each x column has a brick whose lists are full from every q. `donor_block`: holds (i * 16 + j) * 128 + k for a cell of brick (x, q) with i <= 1, j <= 14, k <= 126; entry [x, q, p, s] serves slot s of ghost_cell[x, p, q]; entries of empty slots are arbitrary within the range.
All inputs are finite; a program needn't handle non-finite values.
Results may differ from the reference program's by a relative error of at most 0.0003.
Values sent between devices are 32-bit elements; how exact they have to be, the bound alone decides.
A program may use at most 32 MiB of HBM per device.

```python
import jax
import jax.numpy as jnp
from jax import lax

BX = 3
BY = 16
BZ = 128
CAP = 192
NX = 192
NY = 256
CELLS = 6144
N_GX = 64
N_GY = 16


def draw_state(key, part):
    key = jax.random.fold_in(key, 11)
    subkeys = jax.random.split(key, 3)
    grid_shape = (NX, NY, BZ)
    density = jax.random.uniform(subkeys[0], grid_shape, jnp.float32, 0.6, 1.5)
    velocity = 0.3 * jax.random.truncated_normal(subkeys[1], -2.5, 2.5, (3,) + grid_shape, jnp.float32)
    pressure = jax.random.uniform(subkeys[2], grid_shape, jnp.float32, 0.6, 1.5)
    momenta = density[None] * velocity
    energy = pressure / 0.4 + 0.5 * density * jnp.sum(velocity * velocity, axis=0)
    return jnp.concatenate([density[None], momenta, energy[None]], axis=0)


def draw_ghost_cell(key, part):
    key = jax.random.fold_in(key, 23)
    subkeys = jax.random.split(key, 4)
    hot_row = jax.random.randint(subkeys[0], (N_GX, 1, 1), 0, N_GY)
    owner = jnp.arange(N_GY, dtype=jnp.int32)[None, :, None]
    factor = jnp.maximum(2, 4 - jnp.abs(owner - hot_row))
    load_count = jax.random.randint(subkeys[1], (N_GX, N_GY, N_GY), 0, CAP + 1) * factor // 4
    load_count = jnp.where(owner == hot_row, CAP, load_count)
    slot_count = N_GY * CAP
    bucket = CELLS // slot_count

    def pick_order(subkey):
        return jax.random.permutation(subkey, slot_count)
    shuffled = jax.vmap(pick_order)(jax.random.split(subkeys[2], N_GX * N_GY))
    within = jax.random.randint(subkeys[3], (N_GX * N_GY, slot_count), 0, bucket)
    within = jnp.where(shuffled == 0, 0, within)
    chosen = CELLS - 1 - (shuffled * bucket + within)
    chosen = chosen.reshape(N_GX, N_GY, N_GY, CAP)
    position = jnp.arange(CAP, dtype=jnp.int32)[None, None, None, :]
    return jnp.where(position < load_count[..., None], chosen, -1).astype(jnp.int32)


def draw_donor_block(key, part):
    key = jax.random.fold_in(key, 37)
    subkeys = jax.random.split(key, 3)
    grid_shape = (N_GX, N_GY, N_GY, CAP)
    coord_x = jax.random.randint(subkeys[0], grid_shape, 0, BX - 1)
    coord_y = jax.random.randint(subkeys[1], grid_shape, 0, BY - 1)
    coord_z = jax.random.randint(subkeys[2], grid_shape, 0, BZ - 1)
    return ((coord_x * BY + coord_y) * BZ + coord_z).astype(jnp.int32)


def block_levels(own_key, extent, cuts, low, largest):
    level, own = 1.0, jax.random.fold_in(own_key, 6)
    for dim, parts in cuts:
        heights = jnp.exp(jax.random.uniform(jax.random.fold_in(own, dim), (parts,), jnp.float32, low / len(cuts), largest / len(cuts)))
        level = level * jnp.repeat(heights, extent[dim] // parts).reshape([-1 if axis == dim else 1 for axis in range(len(extent))])
    return level


def setup_inputs(seed: int = 0) -> dict:
    keys = jax.random.split(jax.random.key(seed), 6)
    state = draw_state(jax.random.fold_in(keys[5], 71), 0)
    lf_speed = jnp.clip(jax.random.uniform(keys[1], (3,), jnp.float32, 2.5, 4.0), 2.5, 4.0)
    ghost_cell = draw_ghost_cell(jax.random.fold_in(keys[5], 71), 0)
    ghost_frac = jnp.clip(1.0 * jax.random.uniform(keys[3], (3, N_GX, N_GY, N_GY, CAP), jnp.float32) ** block_levels(keys[3], (3, N_GX, N_GY, N_GY, CAP), ((1, 64), (2, 16)), -0.2, 0.2), 0.0, 1.0)
    donor_block = draw_donor_block(jax.random.fold_in(keys[5], 71), 0)
    return {"state": state, "lf_speed": lf_speed, "ghost_cell": ghost_cell, "ghost_frac": ghost_frac, "donor_block": donor_block}


heat_ratio = 1.4
time_step = 0.25
small_eps = 1e-6
wall_sign = (1.0, -1.0, -1.0, -1.0, 1.0)


def smoothed(far_left, near_left, center, near_right, far_right):
    beta_zero = (13.0 / 12.0) * (far_left - 2.0 * near_left + center) ** 2 + 0.25 * (far_left - 4.0 * near_left + 3.0 * center) ** 2
    beta_one = (13.0 / 12.0) * (near_left - 2.0 * center + near_right) ** 2 + 0.25 * (near_left - near_right) ** 2
    beta_two = (13.0 / 12.0) * (center - 2.0 * near_right + far_right) ** 2 + 0.25 * (3.0 * center - 4.0 * near_right + far_right) ** 2
    weight_zero = 0.1 / (small_eps + beta_zero) ** 2
    weight_one = 0.6 / (small_eps + beta_one) ** 2
    weight_two = 0.3 / (small_eps + beta_two) ** 2
    guess_zero = (2.0 * far_left - 7.0 * near_left + 11.0 * center) / 6.0
    guess_one = (-near_left + 5.0 * center + 2.0 * near_right) / 6.0
    guess_two = (2.0 * center + 5.0 * near_right - far_right) / 6.0
    return (weight_zero * guess_zero + weight_one * guess_one + weight_two * guess_two) / (weight_zero + weight_one + weight_two)


def primitive(conserved):
    density = conserved[0]
    velocity = conserved[1:4] / density[None]
    pressure = (heat_ratio - 1.0) * (conserved[4] - 0.5 * jnp.sum(conserved[1:4] * velocity, axis=0))
    return jnp.concatenate([density[None], velocity, pressure[None]], axis=0)


def flux_change(prim_field, sweep_axis, lf_value, direction):
    density = prim_field[0]
    velocity = prim_field[1:4]
    pressure = prim_field[4]
    normal = velocity[direction]
    energy = pressure / (heat_ratio - 1.0) + 0.5 * density * jnp.sum(velocity * velocity, axis=0)
    momenta = density[None] * velocity
    conserved = jnp.concatenate([density[None], momenta, energy[None]], axis=0)
    momentum_flux = momenta * normal[None]
    momentum_flux = momentum_flux.at[direction].add(pressure)
    fluxes = jnp.concatenate([(density * normal)[None], momentum_flux, (normal * (energy + pressure))[None]], axis=0)
    upwind = 0.5 * (fluxes + lf_value * conserved)
    downwind = 0.5 * (fluxes - lf_value * conserved)
    interior = prim_field.shape[sweep_axis] - 6

    def window(values, offset):
        return lax.slice_in_dim(values, offset, offset + interior + 1, axis=sweep_axis)

    face_flux = smoothed(window(upwind, 0), window(upwind, 1), window(upwind, 2), window(upwind, 3), window(upwind, 4))
    face_flux = face_flux + smoothed(window(downwind, 5), window(downwind, 4), window(downwind, 3), window(downwind, 2), window(downwind, 1))
    return lax.slice_in_dim(face_flux, 1, interior + 1, axis=sweep_axis) - lax.slice_in_dim(face_flux, 0, interior, axis=sweep_axis)


def corner_weights(fractions):
    result = []
    for corner in range(8):
        part_x = fractions[0] if corner // 4 == 1 else 1.0 - fractions[0]
        part_y = fractions[1] if (corner // 2) % 2 == 1 else 1.0 - fractions[1]
        part_z = fractions[2] if corner % 2 == 1 else 1.0 - fractions[2]
        result.append((part_x * part_y) * part_z)
    return result


def reference(state, lf_speed, ghost_cell, ghost_frac, donor_block):
    plane_cells = BY * BZ
    total_cells = NX * NY * BZ
    flat_state = state.reshape(5, total_cells)
    column = jnp.arange(N_GX, dtype=jnp.int32)[:, None, None, None]
    row_owner = jnp.arange(N_GY, dtype=jnp.int32)[None, :, None, None]
    source = jnp.arange(N_GY, dtype=jnp.int32)[None, None, :, None]

    def global_index(local_index, brick_y):
        return ((column * BX + local_index // plane_cells) * NY + brick_y * BY + (local_index // BZ) % BY) * BZ + local_index % BZ

    donors = jnp.swapaxes(donor_block, 1, 2)
    donor_index = global_index(donors, source)
    weights = corner_weights(ghost_frac)
    image_value = jnp.zeros((5,) + donors.shape, jnp.float32)
    for corner in range(8):
        offset = (corner // 4) * NY * BZ + ((corner // 2) % 2) * BZ + corner % 2
        image_value = image_value + weights[corner][None] * flat_state[:, donor_index + offset]
    wall_signs = jnp.array(wall_sign, jnp.float32)[:, None, None, None, None]
    ghost_values = (image_value * wall_signs).reshape(5, -1)
    target = jnp.where(ghost_cell >= 0, global_index(ghost_cell, row_owner), total_cells).reshape(-1)
    filled = flat_state.at[:, target].set(ghost_values, mode="drop").reshape(5, NX, NY, BZ)
    frozen = jnp.zeros((total_cells,), jnp.int32).at[target].set(1, mode="drop").reshape(NX, NY, BZ)

    def slab_update(result, brick_x):
        slab_rows = jnp.clip(brick_x * BX - 3 + jnp.arange(BX + 6, dtype=jnp.int32), 0, NX - 1)
        slab_cells = jnp.take(filled, slab_rows, axis=1)
        slab_cells = jnp.pad(slab_cells, ((0, 0), (0, 0), (3, 3), (3, 3)), mode="edge")
        prim_field = primitive(slab_cells)
        change = flux_change(prim_field[:, :, 3:-3, 3:-3], 1, lf_speed[0], 0)
        change = change + flux_change(prim_field[:, 3:-3, :, 3:-3], 2, lf_speed[1], 1)
        change = change + flux_change(prim_field[:, 3:-3, 3:-3, :], 3, lf_speed[2], 2)
        center = lax.dynamic_slice_in_dim(filled, brick_x * BX, BX, axis=1)
        mask_part = lax.dynamic_slice_in_dim(frozen, brick_x * BX, BX, axis=0)
        updated = jnp.where(mask_part[None] == 1, center, center - time_step * change)
        return lax.dynamic_update_slice_in_dim(result, updated, brick_x * BX, axis=1), None

    result, unused = lax.scan(slab_update, filled, jnp.arange(N_GX, dtype=jnp.int32))
    return result
```

```python
import functools

import jax
import jax.numpy as jnp
from jax import lax
from jax.experimental import pallas as pl
from jax.experimental.pallas import tpu as pltpu
from jax.sharding import PartitionSpec as P

MESH = pl.DeviceIdType.MESH
F32 = jnp.float32
BF16 = jnp.bfloat16
SIGN = (1.0, -1.0, -1.0, -1.0, 1.0)
EPS = 16.0e-6
C13 = 13.0 / 3.0
NX, NY, NZ = 3, 16, 128
ROWS = 24


def loop(count, body):
    def step(i, carry):
        body(i)
        return carry

    lax.fori_loop(0, count, step, 0, unroll=True)


def sq(x):
    return x * x


def rcp(x):
    r = pl.reciprocal(x, approx=True)
    return r * (2.0 - x * r)


def iota(shape, dim):
    return lax.broadcasted_iota(jnp.int32, shape, dim)


def betas(w):
    n = w.shape[0] - 4
    d = w[1:] - w[:-1]
    dd = d[1:] - d[:-1]
    e = (C13 * dd) * dd + EPS
    t = dd[1:] - dd[:-1]
    left = e[:n] + sq(3.0 * d[1 : n + 1] - d[:n])
    mid = e[1 : n + 1] + sq(d[1 : n + 1] + d[2 : n + 2])
    right = e[2 : n + 2] + sq(3.0 * d[2 : n + 2] - d[3 : n + 3])
    return w[2 : n + 2], d[1 : n + 1], d[2 : n + 2], t[:n], t[1:], left, mid, right


def upwind(f, dm, dp, tm, tp, left, mid, right):
    a, b, c = sq(mid * right), sq(left * right), 3.0 * sq(left * mid)
    return 6.0 * f + dm + 2.0 * dp - (2.0 * a * tm + c * tp) * rcp(a + 6.0 * b + c)


def downwind(f, dm, dp, tm, tp, left, mid, right):
    a, b, c = sq(mid * left), sq(left * right), 3.0 * sq(mid * right)
    return 6.0 * f - dp - 2.0 * dm + (2.0 * a * tp + c * tm) * rcp(a + 6.0 * b + c)


def z_change(fp, fm):
    lane = iota(fp.shape, 1)
    first, last = lane == 0, lane == NZ - 1
    down = lambda x: pltpu.roll(x, 1, 1)
    up = lambda x: pltpu.roll(x, NZ - 1, 1)

    def parts(f):
        dp = jnp.where(last, 0.0, up(f) - f)
        dm = down(dp)
        dd = dp - dm
        e = (C13 * dd) * dd + EPS
        left, right = e + sq(3.0 * dp - dm), e + sq(3.0 * dm - dp)
        mid = e + sq(dp + dm)
        tm = dd - jnp.where(first, 0.0, down(dd))
        tp = jnp.where(last, 0.0, up(dd)) - dd
        args = (f, dm, dp, tm, tp, jnp.where(first, EPS, down(left)), mid, jnp.where(last, EPS, up(right)))
        return args, dd, left, right

    plus, dd_plus, _, right = parts(fp)
    minus, dd_minus, left, _ = parts(fm)
    rp, rm = upwind(*plus), downwind(*minus)
    f = jnp.where(first, fp, fm)
    dd = jnp.where(first, dd_plus, dd_minus)
    far = jnp.where(first, right, left)
    edge = 6.0 * f - 3.0 * EPS * EPS * dd * rcp(7.0 * sq(far) + 3.0 * EPS * EPS)
    return rp - jnp.where(first, edge, down(rp)) + jnp.where(last, edge, up(rm)) - rm


def inverse_pressure(u):
    rinv = 1.0 / u[0]
    kinetic = (u[1] * u[1] + u[2] * u[2] + u[3] * u[3]) * rinv
    return rinv, 0.4 * (u[4] - 0.5 * kinetic)


def split(u, rinv, p, direction, speed):
    normal = u[1 + direction] * rinv
    result = []
    for v in range(5):
        if v == 0:
            f = u[1 + direction]
        elif v == 4:
            f = normal * (u[4] + p)
        else:
            f = normal * u[v]
            if v == 1 + direction:
                f = f + p
        s = speed * u[v]
        result.append((f + s, f - s))
    return result


def kernel(
    n_gx, n_gy, lf, state_h, cell_h, frac_h, donor_h, out_h,
    stv, cellv, fracv, donv, fsend, frecv, isend, irecv, kq, cq, fq, ss, pp, bs, ohs, am, maskv,
    fil, xl, xr, yl, yr, fx, fy, fz, fluxy, chg, outv,
    in_sem, fs_sem, fr_sem, is_sem, ir_sem, hs_sem, hr_sem, out_sem,
):
    gx, gy = lax.axis_index("gx"), lax.axis_index("gy")
    right, left = lax.rem(gx + 1, n_gx), lax.rem(gx + n_gx - 1, n_gx)
    above, below = lax.rem(gy + 1, n_gy), lax.rem(gy + n_gy - 1, n_gy)
    low_half = gy < n_gy // 2

    loads = [
        pltpu.make_async_copy(src, dst, in_sem.at[i])
        for i, (src, dst) in enumerate(((frac_h, fracv), (donor_h, donv), (state_h, stv), (cell_h, cellv)))
    ]
    for load in loads:
        load.start()

    barrier = pltpu.get_barrier_semaphore()
    for off in range(1, n_gy):
        pl.semaphore_signal(barrier, inc=1, device_id={"gy": lax.rem(gy + off, n_gy)}, device_id_type=MESH)
    for other in (left, right):
        pl.semaphore_signal(barrier, inc=1, device_id={"gx": other}, device_id_type=MESH)

    def pack(x):
        tail = x[:, 128:192]
        return x[:, 0:128], jnp.concatenate([tail[0:8], tail[8:16]], axis=1)

    loads[0].wait()
    fsend[...] = jnp.zeros_like(fsend)
    for c in range(3):
        main, tail = pack(fracv[c])
        fsend[pl.ds(c, 16, 8), :] = main
        fsend[pl.ds(3 + c, 8, 8), :] = tail
        fsend[pl.ds(64 + 3 + c, 8, 8), :] = tail
    pl.semaphore_wait(barrier, n_gy + 1)

    def exchange(send, recv, rows, s_sem, r_sem):
        copies = []
        mine = pl.ds(pl.multiple_of(gy * rows, 8), rows)
        for off in range(1, n_gy):
            other = lax.rem(gy + off, n_gy)
            copy = pltpu.make_async_remote_copy(
                src_ref=send.at[pl.ds(pl.multiple_of(other * rows, 8), rows), :],
                dst_ref=recv.at[mine, :],
                send_sem=s_sem.at[off - 1],
                recv_sem=r_sem.at[off - 1],
                device_id={"gy": other},
                device_id_type=MESH,
            )
            copy.start()
            copies.append(copy)
        recv[mine, :] = send[mine, :]
        return copies

    frac_copies = exchange(fsend, frecv, 8, fs_sem, fr_sem)

    loads[1].wait()
    main, tail = pack(donv[...])
    kq[...] = jnp.concatenate([main, tail], axis=0)
    loads[2].wait()
    flat = stv[...].reshape(240, 128)
    high = flat.astype(BF16)
    ss[:, 0:128] = high
    ss[:, 128:256] = (flat - high.astype(F32)).astype(BF16)

    def corners(r):
        donor = kq[pl.ds(r, 1), :]
        k = jnp.bitwise_and(donor, 127)
        i0 = jnp.right_shift(donor, 11)
        at = iota((128, 128), 0) - k
        here = jnp.where(at == 0, 1.0, 0.0).astype(F32)
        step = jnp.where(at == 1, 1.0, -here)
        here, step = here.astype(BF16), step.astype(BF16)
        z = jnp.concatenate(
            [jnp.concatenate([here, here], axis=0), jnp.concatenate([step, step], axis=0)], axis=1
        )
        t = jnp.dot(ss[...], z, preferred_element_type=F32)
        for c in range(2):
            tc = t[:, c * 128 : (c + 1) * 128].reshape(5, NX, NY, 128)
            x0 = jnp.where(i0 == 0, tc[:, 0], tc[:, 1])
            x1 = jnp.where(i0 == 0, tc[:, 1], tc[:, 2])
            pp[r, 2 * c] = x0
            pp[r, 2 * c + 1] = x1 - x0

    loop(ROWS, corners)

    def combine(low, high):
        lane = iota((8, 128), 1)
        return jnp.where(
            lane < 64,
            jnp.where(low_half, low, pltpu.roll(low, 64, 1)),
            jnp.where(low_half, pltpu.roll(high, 64, 1), high),
        )

    for copy in frac_copies:
        copy.wait_recv()
    for c in range(3):
        fq[c, 0:16] = frecv[pl.ds(c, 16, 8), :]
        fq[c, 16:24] = combine(frecv[pl.ds(3 + c, 8, 8), :], frecv[pl.ds(64 + 3 + c, 8, 8), :])

    def image(r):
        donor = kq[pl.ds(r, 1), :]
        j0 = jnp.bitwise_and(jnp.right_shift(donor, 7), 15)
        f0, f1, f2 = (fq[c, pl.ds(r, 1), :] for c in range(3))
        at = iota((NY, 128), 0) - j0
        wy = jnp.where(at == 0, 1.0 - f1, jnp.where(at == 1, f1, 0.0))
        value = pp[r, 0] + f0 * pp[r, 1] + f2 * (pp[r, 2] + f0 * pp[r, 3])
        return jnp.sum(value * wy, axis=1)

    def image_main(r):
        isend[pl.ds(pl.multiple_of(r * 16, 16), 5), :] = image(r)

    def image_tail(t):
        value = image(t + 16)
        isend[pl.ds(pl.multiple_of(t * 16, 16) + 8, 5), :] = value
        isend[pl.ds(pl.multiple_of(t * 16, 16) + 136, 5), :] = value

    isend[...] = jnp.zeros_like(isend)
    loop(16, image_main)
    loop(8, image_tail)
    image_copies = exchange(isend, irecv, 16, is_sem, ir_sem)

    loads[3].wait()
    main, tail = pack(cellv[...])
    valid = jnp.concatenate([main, tail], axis=0)
    cq[...] = jnp.where(valid < 0, -4096, valid)

    def places(r):
        cell = cq[pl.ds(r, 1), :]
        j = jnp.right_shift(cell, 7)
        column = jnp.bitwise_or(jnp.bitwise_and(jnp.right_shift(cell, 3), 128), jnp.bitwise_and(cell, 127))
        row = jnp.bitwise_or(jnp.left_shift(jnp.right_shift(cell, 11), 3), jnp.bitwise_and(j, 7))
        bs[:, pl.ds(pl.multiple_of(r * 128, 128), 128)] = jnp.where(iota((256, 128), 0) == column, 1.0, 0.0).astype(BF16)
        i48 = iota((48, 128), 0)
        want = jnp.bitwise_or(jnp.left_shift(jnp.right_shift(i48, 4), 3), jnp.bitwise_and(i48, 7))
        ohs[:, pl.ds(pl.multiple_of(r * 128, 128), 128)] = jnp.where(want == row, 1.0, 0.0).astype(BF16)

    loop(ROWS, places)
    nt = (((1,), (1,)), ((), ()))
    count = lax.dot_general(ohs[...], bs[...], nt, preferred_element_type=F32).reshape(NX, 2, 8, 256)
    maskv[:, 0:8] = count[:, 0, :, 0:128]
    maskv[:, 8:16] = count[:, 0, :, 128:256]

    for copy in image_copies:
        copy.wait_recv()

    def spread(ghost, r):
        where = pl.ds(r * 128, 128)
        rows = ohs[:, where].reshape(NX, 16, 128)
        for v in range(5):
            g = jnp.broadcast_to(SIGN[v] * ghost[v], (8, 128))
            hi = g.astype(BF16)
            lo = (g - hi.astype(F32)).astype(BF16)
            both = jnp.concatenate([hi, lo], axis=0)
            am[v * 48 : (v + 1) * 48, where] = (rows * both[None]).reshape(48, 128)

    for r in range(16):
        spread([irecv[r * 16 + v : r * 16 + v + 1, :] for v in range(5)], r)
    for t in range(8):
        value = combine(irecv[t * 16 + 8 : t * 16 + 16, :], irecv[t * 16 + 136 : t * 16 + 144, :])
        spread([value[v : v + 1] for v in range(5)], 16 + t)
    ghost = lax.dot_general(am[...], bs[...], nt, preferred_element_type=F32).reshape(5, NX, 2, 8, 256)
    ghost = ghost[:, :, 0] + ghost[:, :, 1]
    for half in range(2):
        rows = pl.ds(half * 8, 8)
        fil[:, :, rows] = jnp.where(
            maskv[:, rows][None] > 0.5, ghost[..., half * 128 : (half + 1) * 128], stv[:, :, rows]
        )

    halo_copies = []
    for i, (src, dst, where) in enumerate(
        (
            (fil, xl, {"gx": right}),
            (fil, xr, {"gx": left}),
            (fil.at[:, :, 8:16, :], yl, {"gy": above}),
            (fil.at[:, :, 0:8, :], yr, {"gy": below}),
        )
    ):
        copy = pltpu.make_async_remote_copy(
            src_ref=src, dst_ref=dst, send_sem=hs_sem.at[i], recv_sem=hr_sem.at[i], device_id=where, device_id_type=MESH
        )
        copy.start()
        halo_copies.append(copy)

    u = [fil[v] for v in range(5)]
    rinv, p = inverse_pressure(u)
    for v, pair in enumerate(split(u, rinv, p, 2, lf[2])):
        for s in range(2):
            fz[s, v * NX : (v + 1) * NX] = pair[s]
    for v, pair in enumerate(split(u, rinv, p, 1, lf[1])):
        for s in range(2):
            for i in range(NX):
                fy[pl.ds((s * 32 + 8) * 16 + v * NX + i, 16, 16), :] = pair[s][i]
    for v, pair in enumerate(split(u, rinv, p, 0, lf[0])):
        for s in range(2):
            fx[s, v, 3:6] = pair[s]

    def along_z(n):
        chg[n] = z_change(fz[0, n], fz[1, n])

    loop(15, along_z)

    for copy in halo_copies[2:]:
        copy.wait_recv()
    for edge, ref, row, base in ((gy == 0, yl, 0, 0), (gy == n_gy - 1, yr, 15, 24)):
        u = [jnp.where(edge, fil[v, :, row : row + 1, :], ref[v]) for v in range(5)]
        rinv, p = inverse_pressure(u)
        for v, pair in enumerate(split(u, rinv, p, 1, lf[1])):
            for s in range(2):
                for i in range(NX):
                    fy[pl.ds((s * 32 + base) * 16 + v * NX + i, 8, 16), :] = pair[s][i]

    def along_y(n):
        b, h = n // 2, n % 2

        def window(s, start, count):
            return jnp.stack([fy[pl.ds(pl.multiple_of((s * 32 + start + q) * 16 + h * 8, 8), 8), :] for q in range(count)])

        flux = upwind(*betas(window(0, 5 + 3 * b, 7))) + downwind(*betas(window(1, 6 + 3 * b, 7)))
        for q in range(3):
            fluxy[pl.ds(pl.multiple_of((3 * b + q) * 16 + h * 8, 8), 8), :] = flux[q]

    loop(12, along_y)
    for n in range(15):
        chg[n] = chg[n] + (fluxy[pl.ds(16 + n, 16, 16), :] - fluxy[pl.ds(n, 16, 16), :])

    for copy in halo_copies[:2]:
        copy.wait_recv()
    for edge, ref, row, base in ((gx == 0, xl, 0, 0), (gx == n_gx - 1, xr, 2, 6)):
        u = [jnp.where(edge, fil[v, row : row + 1], ref[v]) for v in range(5)]
        rinv, p = inverse_pressure(u)
        for v, pair in enumerate(split(u, rinv, p, 0, lf[0])):
            for s in range(2):
                fx[s, v, base : base + 3] = pair[s]

    def along_x(n):
        v, h = n // 2, n % 2
        rows = pl.ds(pl.multiple_of(h * 8, 8), 8)
        flux = upwind(*betas(fx[0, v, 0:8, rows])) + downwind(*betas(fx[1, v, 1:9, rows]))
        change = flux[1:] - flux[:-1] + chg[pl.ds(v * NX, NX), rows]
        mine = fil[v, :, rows]
        outv[v, :, rows] = jnp.where(maskv[:, rows] > 0.5, mine, mine - (0.125 / 6.0) * change)

    loop(10, along_x)
    store = pltpu.make_async_copy(outv, out_h, out_sem)
    store.start()
    for copy in frac_copies + image_copies + halo_copies:
        copy.wait_send()
    store.wait()


def solution(mesh):
    n_gx, n_gy = mesh.shape["gx"], mesh.shape["gy"]

    def on_device(state, lf_speed, ghost_cell, ghost_frac, donor_block):
        hbm = pl.BlockSpec(memory_space=pl.ANY)
        vmem = pltpu.VMEM
        dma = pltpu.SemaphoreType.DMA
        brick = (5, NX, NY, NZ)
        return pl.pallas_call(
            functools.partial(kernel, n_gx, n_gy),
            out_shape=jax.ShapeDtypeStruct(brick, F32),
            in_specs=[pl.BlockSpec(memory_space=pltpu.SMEM), hbm, hbm, hbm, hbm],
            out_specs=hbm,
            scratch_shapes=[
                vmem(brick, F32),
                vmem((16, 192), jnp.int32),
                vmem((3, 16, 192), F32),
                vmem((16, 192), jnp.int32),
                vmem((128, 128), F32),
                vmem((128, 128), F32),
                vmem((256, 128), F32),
                vmem((256, 128), F32),
                vmem((ROWS, 128), jnp.int32),
                vmem((ROWS, 128), jnp.int32),
                vmem((3, ROWS, 128), F32),
                vmem((240, 256), BF16),
                vmem((ROWS, 4, 5, NY, 128), F32),
                vmem((256, ROWS * 128), BF16),
                vmem((48, ROWS * 128), BF16),
                vmem((240, ROWS * 128), BF16),
                vmem((NX, NY, NZ), F32),
                vmem(brick, F32),
                vmem(brick, F32),
                vmem(brick, F32),
                vmem((5, NX, 8, NZ), F32),
                vmem((5, NX, 8, NZ), F32),
                vmem((2, 5, 9, NY, NZ), F32),
                vmem((2 * 32 * 16, NZ), F32),
                vmem((2, 15, NY, NZ), F32),
                vmem((18 * 16, NZ), F32),
                vmem((15, NY, NZ), F32),
                vmem(brick, F32),
                dma((4,)),
                dma((n_gy - 1,)),
                dma((n_gy - 1,)),
                dma((n_gy - 1,)),
                dma((n_gy - 1,)),
                dma((4,)),
                dma((4,)),
                dma,
            ],
            compiler_params=pltpu.CompilerParams(
                collective_id=0, has_side_effects=True, vmem_limit_bytes=48 * 1024 * 1024
            ),
        )(
            lf_speed,
            state,
            ghost_cell.reshape(ghost_cell.shape[2:]),
            ghost_frac.reshape((3,) + ghost_frac.shape[3:]),
            donor_block.reshape(donor_block.shape[2:]),
        )

    return jax.shard_map(
        on_device,
        mesh=mesh,
        in_specs=(
            P(None, "gx", "gy", None),
            P(),
            P("gx", "gy", None, None),
            P(None, "gx", "gy", None, None),
            P("gx", "gy", None, None),
        ),
        out_specs=P(None, "gx", "gy", None),
        check_vma=False,
    )
```

```python
import functools

import jax
import jax.numpy as jnp
from jax import lax
from jax.experimental import pallas as pl
from jax.experimental.pallas import tpu as pltpu
from jax.sharding import PartitionSpec as P

MESH = pl.DeviceIdType.MESH
F32 = jnp.float32
BF16 = jnp.bfloat16
SIGN = (1.0, -1.0, -1.0, -1.0, 1.0)
EPS = 16.0e-6
C13 = 13.0 / 3.0
NX, NY, NZ = 3, 16, 128
ROWS = 24


def loop(count, body):
    def step(i, carry):
        body(i)
        return carry

    lax.fori_loop(0, count, step, 0, unroll=True)


def sq(x):
    return x * x


def rcp(x):
    r = pl.reciprocal(x, approx=True)
    return r * (2.0 - x * r)


def iota(shape, dim):
    return lax.broadcasted_iota(jnp.int32, shape, dim)


def betas(w):
    n = w.shape[0] - 4
    d = w[1:] - w[:-1]
    dd = d[1:] - d[:-1]
    e = (C13 * dd) * dd + EPS
    t = dd[1:] - dd[:-1]
    left = e[:n] + sq(3.0 * d[1 : n + 1] - d[:n])
    mid = e[1 : n + 1] + sq(d[1 : n + 1] + d[2 : n + 2])
    right = e[2 : n + 2] + sq(3.0 * d[2 : n + 2] - d[3 : n + 3])
    return w[2 : n + 2], d[1 : n + 1], d[2 : n + 2], t[:n], t[1:], left, mid, right


def upwind(f, dm, dp, tm, tp, left, mid, right):
    a, b, c = sq(mid * right), sq(left * right), 3.0 * sq(left * mid)
    return 6.0 * f + dm + 2.0 * dp - (2.0 * a * tm + c * tp) * rcp(a + 6.0 * b + c)


def downwind(f, dm, dp, tm, tp, left, mid, right):
    a, b, c = sq(mid * left), sq(left * right), 3.0 * sq(mid * right)
    return 6.0 * f - dp - 2.0 * dm + (2.0 * a * tp + c * tm) * rcp(a + 6.0 * b + c)


def z_change(fp, fm):
    lane = iota(fp.shape, 1)
    first, last = lane == 0, lane == NZ - 1
    down = lambda x: pltpu.roll(x, 1, 1)
    up = lambda x: pltpu.roll(x, NZ - 1, 1)

    def parts(f):
        dp = jnp.where(last, 0.0, up(f) - f)
        dm = down(dp)
        dd = dp - dm
        e = (C13 * dd) * dd + EPS
        left, right = e + sq(3.0 * dp - dm), e + sq(3.0 * dm - dp)
        mid = e + sq(dp + dm)
        tm = dd - jnp.where(first, 0.0, down(dd))
        tp = jnp.where(last, 0.0, up(dd)) - dd
        args = (f, dm, dp, tm, tp, jnp.where(first, EPS, down(left)), mid, jnp.where(last, EPS, up(right)))
        return args, dd, left, right

    plus, dd_plus, _, right = parts(fp)
    minus, dd_minus, left, _ = parts(fm)
    rp, rm = upwind(*plus), downwind(*minus)
    f = jnp.where(first, fp, fm)
    dd = jnp.where(first, dd_plus, dd_minus)
    far = jnp.where(first, right, left)
    edge = 6.0 * f - 3.0 * EPS * EPS * dd * rcp(7.0 * sq(far) + 3.0 * EPS * EPS)
    return rp - jnp.where(first, edge, down(rp)) + jnp.where(last, edge, up(rm)) - rm


def inverse_pressure(u):
    rinv = 1.0 / u[0]
    kinetic = (u[1] * u[1] + u[2] * u[2] + u[3] * u[3]) * rinv
    return rinv, 0.4 * (u[4] - 0.5 * kinetic)


def split(u, rinv, p, direction, speed):
    normal = u[1 + direction] * rinv
    result = []
    for v in range(5):
        if v == 0:
            f = u[1 + direction]
        elif v == 4:
            f = normal * (u[4] + p)
        else:
            f = normal * u[v]
            if v == 1 + direction:
                f = f + p
        s = speed * u[v]
        result.append((f + s, f - s))
    return result


def kernel(
    n_gx, n_gy, lf_h, state_h, cell_h, frac_h, donor_h, out_h,
    stv, cellv, fracv, donv, fsend, frecv, isend, irecv, kq, cq, fq, ss, pp, bs, ohs, am, maskv,
    fil, xl, xr, yl, yr, fx, fy, fz, fluxy, chg, outv, lf,
    in_sem, fs_sem, fr_sem, is_sem, ir_sem, hs_sem, hr_sem, out_sem,
):
    gx, gy = lax.axis_index("gx"), lax.axis_index("gy")
    right, left, above, below = gx + 1, gx - 1, gy + 1, gy - 1
    has_left, has_right, has_below, has_above = gx > 0, gx < n_gx - 1, gy > 0, gy < n_gy - 1
    half = iota((1, 128), 1) < 64

    loads = [
        pltpu.make_async_copy(src, dst, in_sem.at[i])
        for i, (src, dst) in enumerate(((frac_h, fracv), (donor_h, donv), (state_h, stv), (cell_h, cellv), (lf_h, lf)))
    ]
    for load in loads:
        load.start()

    barrier = pltpu.get_barrier_semaphore()
    for off in sorted(range(1, n_gy), key=lambda off: -min(off, n_gy - off)):
        pl.semaphore_signal(barrier, inc=1, device_id={"gy": lax.rem(gy + off, n_gy)}, device_id_type=MESH)
    for inside, other in ((has_left, left), (has_right, right)):

        @pl.when(inside)
        def _():
            pl.semaphore_signal(barrier, inc=1, device_id={"gx": other}, device_id_type=MESH)


    def pack(x):
        tail = x[:, 128:192]
        return x[:, 0:128], jnp.concatenate([tail[0:8], tail[8:16]], axis=1)

    def turn(x):
        return pltpu.roll(x, 64, 1)

    def share(tails):
        low = [jnp.where(half, a, turn(b)) for a, b in zip(tails[0::2], tails[1::2])]
        high = [jnp.where(half, turn(a), b) for a, b in zip(tails[0::2], tails[1::2])]
        return low + [tails[-1]], high + [turn(tails[-1])]

    def unshare(low, high):
        rows = []
        for a, b in zip(low, high):
            rows += [jnp.where(half, a, turn(b)), jnp.where(half, turn(a), b)]
        return rows[:-1]

    loads[0].wait()
    fsend[...] = jnp.zeros_like(fsend)
    tails = []
    for c in range(3):
        main, tail = pack(fracv[c])
        fsend[pl.ds(c, 16, 8), :] = main
        tails.append(tail)
    low, high = share(tails)
    for c in range(2):
        fsend[pl.ds(3 + c, 8, 8), :] = low[c]
        fsend[pl.ds(64 + 3 + c, 8, 8), :] = high[c]
    pl.semaphore_wait(barrier, n_gy - 1 + has_left.astype(jnp.int32) + has_right.astype(jnp.int32))

    far = sorted(range(1, n_gy), key=lambda off: -min(off, n_gy - off))

    def exchange(send, recv, rows, s_sem, r_sem):
        copies = []
        mine = pl.ds(pl.multiple_of(gy * rows, 8), rows)
        for off in far:
            other = lax.rem(gy + off, n_gy)
            copy = pltpu.make_async_remote_copy(
                src_ref=send.at[pl.ds(pl.multiple_of(other * rows, 8), rows), :],
                dst_ref=recv.at[mine, :],
                send_sem=s_sem.at[off - 1],
                recv_sem=r_sem.at[off - 1],
                device_id={"gy": other},
                device_id_type=MESH,
            )
            copy.start()
            copies.append(copy)
        recv[mine, :] = send[mine, :]
        return copies

    frac_copies = exchange(fsend, frecv, 8, fs_sem, fr_sem)

    loads[1].wait()
    main, tail = pack(donv[...])
    kq[...] = jnp.concatenate([main, tail], axis=0)
    loads[2].wait()
    flat = stv[...].reshape(240, 128)
    high = flat.astype(BF16)
    ss[:, 0:128] = high
    ss[:, 128:256] = (flat - high.astype(F32)).astype(BF16)

    def corners(r):
        donor = kq[pl.ds(r, 1), :]
        k = jnp.bitwise_and(donor, 127)
        i0 = jnp.right_shift(donor, 11)
        at = iota((128, 128), 0) - k
        here = jnp.where(at == 0, 1.0, 0.0).astype(F32)
        step = jnp.where(at == 1, 1.0, -here)
        here, step = here.astype(BF16), step.astype(BF16)
        z = jnp.concatenate(
            [jnp.concatenate([here, here], axis=0), jnp.concatenate([step, step], axis=0)], axis=1
        )
        t = jnp.dot(ss[...], z, preferred_element_type=F32)
        for c in range(2):
            tc = t[:, c * 128 : (c + 1) * 128].reshape(5, NX, NY, 128)
            x0 = jnp.where(i0 == 0, tc[:, 0], tc[:, 1])
            x1 = jnp.where(i0 == 0, tc[:, 1], tc[:, 2])
            pp[r, 2 * c] = x0
            pp[r, 2 * c + 1] = x1 - x0

    loop(ROWS, corners)

    for copy in frac_copies:
        copy.wait_recv()
    for c in range(3):
        fq[c, 0:16] = frecv[pl.ds(c, 16, 8), :]
    tails = unshare(
        [frecv[pl.ds(3 + c, 8, 8), :] for c in range(2)], [frecv[pl.ds(67 + c, 8, 8), :] for c in range(2)]
    )
    for c in range(3):
        fq[c, 16:24] = tails[c]

    def image(r):
        donor = kq[pl.ds(r, 1), :]
        j0 = jnp.bitwise_and(jnp.right_shift(donor, 7), 15)
        f0, f1, f2 = (fq[c, pl.ds(r, 1), :] for c in range(3))
        at = iota((NY, 128), 0) - j0
        wy = jnp.where(at == 0, 1.0 - f1, jnp.where(at == 1, f1, 0.0))
        value = pp[r, 0] + f0 * pp[r, 1] + f2 * (pp[r, 2] + f0 * pp[r, 3])
        return jnp.sum(value * wy, axis=1)

    def image_main(r):
        isend[pl.ds(pl.multiple_of(r * 8, 8), 5), :] = image(r)

    def image_tail(t):
        value = image(t + 16)
        low, high = share([value[v : v + 1] for v in range(5)])
        for c in range(3):
            isend[pl.ds(pl.multiple_of(t * 8, 8) + 5 + c, 1), :] = low[c]
            isend[pl.ds(pl.multiple_of(t * 8, 8) + 69 + c, 1), :] = high[c]

    loop(16, image_main)
    loop(8, image_tail)
    image_copies = exchange(isend, irecv, 8, is_sem, ir_sem)

    loads[3].wait()
    loads[4].wait()
    main, tail = pack(cellv[...])
    valid = jnp.concatenate([main, tail], axis=0)
    cq[...] = jnp.where(valid < 0, -4096, valid)

    def places(r):
        cell = cq[pl.ds(r, 1), :]
        j = jnp.right_shift(cell, 7)
        column = jnp.bitwise_or(jnp.bitwise_and(jnp.right_shift(cell, 3), 128), jnp.bitwise_and(cell, 127))
        row = jnp.bitwise_or(jnp.left_shift(jnp.right_shift(cell, 11), 3), jnp.bitwise_and(j, 7))
        bs[:, pl.ds(pl.multiple_of(r * 128, 128), 128)] = jnp.where(iota((256, 128), 0) == column, 1.0, 0.0).astype(BF16)
        i48 = iota((48, 128), 0)
        want = jnp.bitwise_or(jnp.left_shift(jnp.right_shift(i48, 4), 3), jnp.bitwise_and(i48, 7))
        ohs[:, pl.ds(pl.multiple_of(r * 128, 128), 128)] = jnp.where(want == row, 1.0, 0.0).astype(BF16)

    loop(ROWS, places)
    nt = (((1,), (1,)), ((), ()))
    count = lax.dot_general(ohs[...], bs[...], nt, preferred_element_type=F32).reshape(NX, 2, 8, 256)
    maskv[:, 0:8] = count[:, 0, :, 0:128]
    maskv[:, 8:16] = count[:, 0, :, 128:256]

    for copy in image_copies:
        copy.wait_recv()

    def spread(ghost, r):
        where = pl.ds(r * 128, 128)
        rows = ohs[:, where].reshape(NX, 16, 128)
        for v in range(5):
            g = jnp.broadcast_to(SIGN[v] * ghost[v], (8, 128))
            hi = g.astype(BF16)
            lo = (g - hi.astype(F32)).astype(BF16)
            both = jnp.concatenate([hi, lo], axis=0)
            am[v * 48 : (v + 1) * 48, where] = (rows * both[None]).reshape(48, 128)

    for r in range(16):
        spread([irecv[r * 8 + v : r * 8 + v + 1, :] for v in range(5)], r)
    for t in range(8):
        low, high = ([irecv[b + 5 + c : b + 6 + c, :] for c in range(3)] for b in (t * 8, t * 8 + 64))
        spread(unshare(low, high), 16 + t)
    ghost = lax.dot_general(am[...], bs[...], nt, preferred_element_type=F32).reshape(5, NX, 2, 8, 256)
    ghost = ghost[:, :, 0] + ghost[:, :, 1]
    for half in range(2):
        rows = pl.ds(half * 8, 8)
        fil[:, :, rows] = jnp.where(
            maskv[:, rows][None] > 0.5, ghost[..., half * 128 : (half + 1) * 128], stv[:, :, rows]
        )

    halos = {
        name: (
            pltpu.make_async_remote_copy(
                src_ref=src, dst_ref=dst, send_sem=hs_sem.at[i], recv_sem=hr_sem.at[i], device_id=where, device_id_type=MESH
            ),
            sends,
            receives,
        )
        for i, (name, src, dst, where, sends, receives) in enumerate(
            (
                ("xl", fil, xl, {"gx": right}, has_right, has_left),
                ("xr", fil, xr, {"gx": left}, has_left, has_right),
                ("yl", fil.at[:, :, 8:16, :], yl, {"gy": above}, has_above, has_below),
                ("yr", fil.at[:, :, 0:8, :], yr, {"gy": below}, has_below, has_above),
            )
        )
    }
    for copy, sends, _ in halos.values():
        pl.when(sends)(copy.start)

    def arrived(*names):
        for name in names:
            copy, _, receives = halos[name]
            pl.when(receives)(copy.wait_recv)

    u = [fil[v] for v in range(5)]
    rinv, p = inverse_pressure(u)
    for v, pair in enumerate(split(u, rinv, p, 2, lf[2])):
        for s in range(2):
            fz[s, v * NX : (v + 1) * NX] = pair[s]
    for v, pair in enumerate(split(u, rinv, p, 1, lf[1])):
        for s in range(2):
            for i in range(NX):
                fy[pl.ds((s * 32 + 8) * 16 + v * NX + i, 16, 16), :] = pair[s][i]
    for v, pair in enumerate(split(u, rinv, p, 0, lf[0])):
        for s in range(2):
            fx[s, v, 3:6] = pair[s]

    def along_z(n):
        chg[n] = z_change(fz[0, n], fz[1, n])

    loop(15, along_z)

    arrived("yl", "yr")
    for edge, ref, row, base in ((~has_below, yl, 0, 0), (~has_above, yr, 15, 24)):
        u = [jnp.where(edge, fil[v, :, row : row + 1, :], ref[v]) for v in range(5)]
        rinv, p = inverse_pressure(u)
        for v, pair in enumerate(split(u, rinv, p, 1, lf[1])):
            for s in range(2):
                for i in range(NX):
                    fy[pl.ds((s * 32 + base) * 16 + v * NX + i, 8, 16), :] = pair[s][i]

    def along_y(n):
        b, h = n // 2, n % 2

        def window(s, start, count):
            return jnp.stack([fy[pl.ds(pl.multiple_of((s * 32 + start + q) * 16 + h * 8, 8), 8), :] for q in range(count)])

        flux = upwind(*betas(window(0, 5 + 3 * b, 7))) + downwind(*betas(window(1, 6 + 3 * b, 7)))
        for q in range(3):
            fluxy[pl.ds(pl.multiple_of((3 * b + q) * 16 + h * 8, 8), 8), :] = flux[q]

    loop(12, along_y)
    for n in range(15):
        chg[n] = chg[n] + (fluxy[pl.ds(16 + n, 16, 16), :] - fluxy[pl.ds(n, 16, 16), :])

    arrived("xl", "xr")
    for edge, ref, row, base in ((~has_left, xl, 0, 0), (~has_right, xr, 2, 6)):
        u = [jnp.where(edge, fil[v, row : row + 1], ref[v]) for v in range(5)]
        rinv, p = inverse_pressure(u)
        for v, pair in enumerate(split(u, rinv, p, 0, lf[0])):
            for s in range(2):
                fx[s, v, base : base + 3] = pair[s]

    def along_x(n):
        v, h = n // 2, n % 2
        rows = pl.ds(pl.multiple_of(h * 8, 8), 8)
        flux = upwind(*betas(fx[0, v, 0:8, rows])) + downwind(*betas(fx[1, v, 1:9, rows]))
        change = flux[1:] - flux[:-1] + chg[pl.ds(v * NX, NX), rows]
        mine = fil[v, :, rows]
        outv[v, :, rows] = jnp.where(maskv[:, rows] > 0.5, mine, mine - (0.125 / 6.0) * change)

    loop(10, along_x)
    store = pltpu.make_async_copy(outv, out_h, out_sem)
    store.start()
    for copy in frac_copies + image_copies:
        copy.wait_send()
    for copy, sends, _ in halos.values():
        pl.when(sends)(copy.wait_send)
    store.wait()


def solution(mesh):
    n_gx, n_gy = mesh.shape["gx"], mesh.shape["gy"]

    def on_device(state, lf_speed, ghost_cell, ghost_frac, donor_block):
        hbm = pl.BlockSpec(memory_space=pl.ANY)
        vmem = pltpu.VMEM
        dma = pltpu.SemaphoreType.DMA
        brick = (5, NX, NY, NZ)
        return pl.pallas_call(
            functools.partial(kernel, n_gx, n_gy),
            out_shape=jax.ShapeDtypeStruct(brick, F32),
            in_specs=[hbm] * 5,
            out_specs=hbm,
            scratch_shapes=[
                vmem(brick, F32),
                vmem((16, 192), jnp.int32),
                vmem((3, 16, 192), F32),
                vmem((16, 192), jnp.int32),
                vmem((128, 128), F32),
                vmem((128, 128), F32),
                vmem((128, 128), F32),
                vmem((128, 128), F32),
                vmem((ROWS, 128), jnp.int32),
                vmem((ROWS, 128), jnp.int32),
                vmem((3, ROWS, 128), F32),
                vmem((240, 256), BF16),
                vmem((ROWS, 4, 5, NY, 128), F32),
                vmem((256, ROWS * 128), BF16),
                vmem((48, ROWS * 128), BF16),
                vmem((240, ROWS * 128), BF16),
                vmem((NX, NY, NZ), F32),
                vmem(brick, F32),
                vmem(brick, F32),
                vmem(brick, F32),
                vmem((5, NX, 8, NZ), F32),
                vmem((5, NX, 8, NZ), F32),
                vmem((2, 5, 9, NY, NZ), F32),
                vmem((2 * 32 * 16, NZ), F32),
                vmem((2, 15, NY, NZ), F32),
                vmem((18 * 16, NZ), F32),
                vmem((15, NY, NZ), F32),
                vmem(brick, F32),
                pltpu.SMEM((3,), F32),
                dma((5,)),
                dma((n_gy - 1,)),
                dma((n_gy - 1,)),
                dma((n_gy - 1,)),
                dma((n_gy - 1,)),
                dma((4,)),
                dma((4,)),
                dma,
            ],
            compiler_params=pltpu.CompilerParams(
                collective_id=0, has_side_effects=True, vmem_limit_bytes=63 * 1024 * 1024
            ),
        )(
            lf_speed,
            state,
            ghost_cell.reshape(ghost_cell.shape[2:]),
            ghost_frac.reshape((3,) + ghost_frac.shape[3:]),
            donor_block.reshape(donor_block.shape[2:]),
        )

    return jax.shard_map(
        on_device,
        mesh=mesh,
        in_specs=(
            P(None, "gx", "gy", None),
            P(),
            P("gx", "gy", None, None),
            P(None, "gx", "gy", None, None),
            P("gx", "gy", None, None),
        ),
        out_specs=P(None, "gx", "gy", None),
        check_vma=False,
    )
```

```python
import functools

import jax
import jax.numpy as jnp
from jax import lax
from jax.experimental import pallas as pl
from jax.experimental.pallas import tpu as pltpu
from jax.sharding import PartitionSpec as P

MESH = pl.DeviceIdType.MESH
F32 = jnp.float32
BF16 = jnp.bfloat16
SIGN = (1.0, -1.0, -1.0, -1.0, 1.0)
EPS = 16.0e-6
C13 = 13.0 / 3.0
NX, NY, NZ = 3, 16, 128
ROWS = 24


def loop(count, body):
    def step(i, carry):
        body(i)
        return carry

    lax.fori_loop(0, count, step, 0, unroll=True)


def sq(x):
    return x * x


def rcp(x):
    r = pl.reciprocal(x, approx=True)
    return r * (2.0 - x * r)


def iota(shape, dim):
    return lax.broadcasted_iota(jnp.int32, shape, dim)


def betas(w):
    n = w.shape[0] - 4
    d = w[1:] - w[:-1]
    dd = d[1:] - d[:-1]
    e = (C13 * dd) * dd + EPS
    t = dd[1:] - dd[:-1]
    left = e[:n] + sq(3.0 * d[1 : n + 1] - d[:n])
    mid = e[1 : n + 1] + sq(d[1 : n + 1] + d[2 : n + 2])
    right = e[2 : n + 2] + sq(3.0 * d[2 : n + 2] - d[3 : n + 3])
    return w[2 : n + 2], d[1 : n + 1], d[2 : n + 2], t[:n], t[1:], left, mid, right


def upwind(f, dm, dp, tm, tp, left, mid, right):
    a, b, c = sq(mid * right), sq(left * right), 3.0 * sq(left * mid)
    return 6.0 * f + dm + 2.0 * dp - (2.0 * a * tm + c * tp) * rcp(a + 6.0 * b + c)


def downwind(f, dm, dp, tm, tp, left, mid, right):
    a, b, c = sq(mid * left), sq(left * right), 3.0 * sq(mid * right)
    return 6.0 * f - dp - 2.0 * dm + (2.0 * a * tp + c * tm) * rcp(a + 6.0 * b + c)


def z_change(fp, fm):
    lane = iota(fp.shape, 1)
    first, last = lane == 0, lane == NZ - 1
    down = lambda x: pltpu.roll(x, 1, 1)
    up = lambda x: pltpu.roll(x, NZ - 1, 1)

    def parts(f):
        dp = jnp.where(last, 0.0, up(f) - f)
        dm = down(dp)
        dd = dp - dm
        e = (C13 * dd) * dd + EPS
        left, right = e + sq(3.0 * dp - dm), e + sq(3.0 * dm - dp)
        mid = e + sq(dp + dm)
        tm = dd - jnp.where(first, 0.0, down(dd))
        tp = jnp.where(last, 0.0, up(dd)) - dd
        args = (f, dm, dp, tm, tp, jnp.where(first, EPS, down(left)), mid, jnp.where(last, EPS, up(right)))
        return args, dd, left, right

    plus, dd_plus, _, right = parts(fp)
    minus, dd_minus, left, _ = parts(fm)
    rp, rm = upwind(*plus), downwind(*minus)
    f = jnp.where(first, fp, fm)
    dd = jnp.where(first, dd_plus, dd_minus)
    far = jnp.where(first, right, left)
    edge = 6.0 * f - 3.0 * EPS * EPS * dd * rcp(7.0 * sq(far) + 3.0 * EPS * EPS)
    return rp - jnp.where(first, edge, down(rp)) + jnp.where(last, edge, up(rm)) - rm


def inverse_pressure(u):
    rinv = 1.0 / u[0]
    kinetic = (u[1] * u[1] + u[2] * u[2] + u[3] * u[3]) * rinv
    return rinv, 0.4 * (u[4] - 0.5 * kinetic)


def split(u, rinv, p, direction, speed):
    normal = u[1 + direction] * rinv
    result = []
    for v in range(5):
        if v == 0:
            f = u[1 + direction]
        elif v == 4:
            f = normal * (u[4] + p)
        else:
            f = normal * u[v]
            if v == 1 + direction:
                f = f + p
        s = speed * u[v]
        result.append((f + s, f - s))
    return result


OTHER = [8, 15, 14, 13, 12, 11, 10, 9]
NEAR = [0, 1, 2, 3, 4, 5, 11, 12, 13, 14, 15, 16 + 1, 16 + 2, 16 + 3, 16 + 4, 16 + 5]
FAR = [6, 7, 8, 9, 10, 16 + 6, 16 + 7, 16 + 0]
ORDER = NEAR + FAR
PLACE = {row: place for place, row in enumerate(ORDER)}
PARTS = (slice(0, 6), slice(11, 16), slice(6, 11))


def kernel(
    n_gx, n_gy, lf_h, state_h, cell_h, frac_h, donor_h, out,
    stv, cellv, fracv, donv, fsend, frecv, isend, irecv, kq, cq, ss, pp, bs, ohs, am, maskv, part,
    fil, yl, yr, fx, fy, fz, fluxy, chg, lf,
    in_sem, fs_sem, fr_sem, is_sem, ir_sem, hs_sem, hr_sem, xs_sem, xr_sem,
):
    gx, gy = lax.axis_index("gx"), lax.axis_index("gy")
    right, left, above, below = gx + 1, gx - 1, gy + 1, gy - 1
    has_left, has_right, has_below, has_above = gx > 0, gx < n_gx - 1, gy > 0, gy < n_gy - 1
    half = iota((1, 128), 1) < 64

    loads = [
        pltpu.make_async_copy(src, dst, in_sem.at[i])
        for i, (src, dst) in enumerate(
            ((frac_h, fracv), (donor_h, donv), (state_h, stv.at[0]), (cell_h, cellv), (lf_h, lf))
        )
    ]
    for load in loads:
        load.start()

    def partner(off):
        return lax.rem(gy + off, n_gy)

    barrier = pltpu.get_barrier_semaphore()
    for off in sorted(range(1, n_gy), key=lambda off: -min(off, n_gy - off)):
        pl.semaphore_signal(barrier, inc=1, device_id={"gy": partner(off)}, device_id_type=MESH)
    for inside, other in ((has_left, left), (has_right, right)):

        @pl.when(inside)
        def _():
            pl.semaphore_signal(barrier, inc=1, device_id={"gx": other}, device_id_type=MESH)

    def turn(x):
        return pltpu.roll(x, 64, x.ndim - 1)

    def share(tails):
        low = [jnp.where(half, a, turn(b)) for a, b in zip(tails[0::2], tails[1::2])]
        high = [jnp.where(half, turn(a), b) for a, b in zip(tails[0::2], tails[1::2])]
        return low + [tails[-1]], high + [turn(tails[-1])]

    def unshare(low, high):
        rows = []
        for a, b in zip(low, high):
            rows += [jnp.where(half, a, turn(b)), jnp.where(half, turn(a), b)]
        return rows[:-1]

    def by_distance(ref, *lead):
        rows = jnp.concatenate([ref[(*lead, pl.ds(partner(off), 1))] for off in range(16)], axis=0)
        tail = rows[:, 128:192]
        high = jnp.concatenate([tail[off : off + 1] for off in OTHER], axis=0)
        return rows[:, 0:128], jnp.concatenate([tail[0:8], high], axis=1)

    loads[0].wait()
    fsend[...] = jnp.zeros_like(fsend)
    tails = []
    for c in range(3):
        main, tail = by_distance(fracv, c)
        fsend[pl.ds(c, 16, 8), :] = main
        tails.append(tail)
    low, high = share(tails)
    for c in range(2):
        fsend[pl.ds(3 + c, 8, 8), :] = low[c]
        for t, off in enumerate(OTHER):
            fsend[off * 8 + 3 + c : off * 8 + 4 + c, :] = high[c][t : t + 1]
    pl.semaphore_wait(barrier, n_gy - 1 + has_left.astype(jnp.int32) + has_right.astype(jnp.int32))

    def message(send, recv, off, s_sem, r_sem):
        copy = pltpu.make_async_remote_copy(
            src_ref=send.at[pl.ds(off * 8, 8), :],
            dst_ref=recv.at[pl.ds((n_gy - off) * 8, 8), :],
            send_sem=s_sem.at[off - 1],
            recv_sem=r_sem.at[n_gy - off - 1],
            device_id={"gy": partner(off)},
            device_id_type=MESH,
        )
        copy.start()
        return copy

    def from_source(copies):
        return {n_gy - off: copy for off, copy in copies.items()}

    offs = [off for t in (0, 7, 6, 5, 4, 3, 2, 1) for off in (OTHER[t], t) if off]
    frac_copies = {off: message(fsend, frecv, off, fs_sem, fr_sem) for off in offs}
    frecv[0:8] = fsend[0:8]

    def beside(src, dsts, i):
        result = []
        for side, (other, sends, receives) in enumerate(((right, has_right, has_left), (left, has_left, has_right))):
            copy = pltpu.make_async_remote_copy(
                src_ref=src,
                dst_ref=dsts[side],
                send_sem=xs_sem.at[2 * i + side],
                recv_sem=xr_sem.at[2 * i + side],
                device_id={"gx": other},
                device_id_type=MESH,
            )
            pl.when(sends)(copy.start)
            result.append((copy, sends, receives))
        return result

    def arrived(copies):
        for copy, _, receives in copies:
            pl.when(receives)(copy.wait_recv)

    loads[3].wait()
    loads[2].wait()
    main, tail = by_distance(cellv)
    packed = jnp.concatenate([main, tail], axis=0)
    cq[0] = jnp.where(packed < 0, -4096, packed)
    list_copies = beside(cq.at[0], [cq.at[1], cq.at[2]], 0)

    loads[1].wait()
    main, tail = by_distance(donv)
    kq[...] = jnp.concatenate([main, tail], axis=0)
    flat = stv[0].reshape(240, 128)
    high = flat.astype(BF16)
    ss[:, 0:128] = high
    ss[:, 128:256] = (flat - high.astype(F32)).astype(BF16)

    def corners(r):
        donor = kq[pl.ds(r, 1), :]
        k = jnp.bitwise_and(donor, 127)
        i0 = jnp.right_shift(donor, 11)
        at = iota((128, 128), 0) - k
        here = jnp.where(at == 0, 1.0, 0.0).astype(F32)
        step = jnp.where(at == 1, 1.0, -here)
        here, step = here.astype(BF16), step.astype(BF16)
        z = jnp.concatenate(
            [jnp.concatenate([here, here], axis=0), jnp.concatenate([step, step], axis=0)], axis=1
        )
        t = jnp.dot(ss[...], z, preferred_element_type=F32)
        for c in range(2):
            tc = t[:, c * 128 : (c + 1) * 128].reshape(5, NX, NY, 128)
            x0 = jnp.where(i0 == 0, tc[:, 0], tc[:, 1])
            x1 = jnp.where(i0 == 0, tc[:, 1], tc[:, 2])
            pp[r, 2 * c] = x0
            pp[r, 2 * c + 1] = x1 - x0

    loop(ROWS, corners)

    def image(r, f0, f1, f2):
        donor = kq[r : r + 1, :]
        j0 = jnp.bitwise_and(jnp.right_shift(donor, 7), 15)
        at = iota((NY, 128), 0) - j0
        wy = jnp.where(at == 0, 1.0 - f1, jnp.where(at == 1, f1, 0.0))
        value = pp[r, 0] + f0 * pp[r, 1] + f2 * (pp[r, 2] + f0 * pp[r, 3])
        return jnp.sum(value * wy, axis=1)

    def row_of(ref, off, c):
        return ref[off * 8 + c : off * 8 + c + 1, :]

    sources = from_source(frac_copies)
    image_copies = {}
    for t in (1, 2, 3, 4, 5, 6, 7, 0):
        both = (OTHER[t], t)
        for off in both:
            if off:
                sources[off].wait_recv()
        for off in both:
            isend[off * 8 : off * 8 + 5, :] = image(off, *(row_of(frecv, off, c) for c in range(3)))
        fracs = unshare(*([row_of(frecv, off, 3 + c) for c in range(2)] for off in (t, OTHER[t])))
        value = image(16 + t, *fracs)
        low, high = share([value[v : v + 1] for v in range(5)])
        for c in range(3):
            isend[t * 8 + 5 + c : t * 8 + 6 + c, :] = low[c]
            isend[OTHER[t] * 8 + 5 + c : OTHER[t] * 8 + 6 + c, :] = high[c]
        for off in both:
            if off:
                image_copies[off] = message(isend, irecv.at[0], off, is_sem, ir_sem)
    irecv[0, 0:8] = isend[0:8]
    by_source = from_source(image_copies)
    raw_copies = beside(stv.at[0], [stv.at[1], stv.at[2]], 1)

    loads[4].wait()
    nt = (((1,), (1,)), ((), ()))

    def places(b):
        for row in range(ROWS):
            where = slice(PLACE[row] * 128, PLACE[row] * 128 + 128)
            cell = cq[b, row : row + 1, :]
            j = jnp.right_shift(cell, 7)
            column = jnp.bitwise_or(jnp.bitwise_and(jnp.right_shift(cell, 3), 128), jnp.bitwise_and(cell, 127))
            line = jnp.bitwise_or(jnp.left_shift(jnp.right_shift(cell, 11), 3), jnp.bitwise_and(j, 7))
            bs[b, :, where] = jnp.where(iota((256, 128), 0) == column, 1.0, 0.0).astype(BF16)
            i48 = iota((48, 128), 0)
            want = jnp.bitwise_or(jnp.left_shift(jnp.right_shift(i48, 4), 3), jnp.bitwise_and(i48, 7))
            ohs[b, :, where] = jnp.where(want == line, 1.0, 0.0).astype(BF16)
        count = lax.dot_general(ohs[b], bs[b], nt, preferred_element_type=F32).reshape(NX, 2, 8, 256)
        maskv[b, :, 0:8] = count[:, 0, :, 0:128]
        maskv[b, :, 8:16] = count[:, 0, :, 128:256]

    def spread(b, rows):
        for row in rows:
            where = slice(PLACE[row] * 128, PLACE[row] * 128 + 128)
            if row < 16:
                ghost = [irecv[b, row * 8 + v : row * 8 + v + 1, :] for v in range(5)]
            else:
                ends = (row - 16, OTHER[row - 16])
                low, high = ([irecv[b, a * 8 + 5 + c : a * 8 + 6 + c, :] for c in range(3)] for a in ends)
                ghost = unshare(low, high)
            lines = ohs[b, :, where].reshape(NX, 16, 128)
            for v in range(5):
                g = jnp.broadcast_to(SIGN[v] * ghost[v], (8, 128))
                hi = g.astype(BF16)
                lo = (g - hi.astype(F32)).astype(BF16)
                both = jnp.concatenate([hi, lo], axis=0)
                am[b, v * 48 : (v + 1) * 48, where] = (lines * both[None]).reshape(48, 128)

    def collect(b, rows):
        where = slice(PLACE[rows[0]] * 128, (PLACE[rows[-1]] + 1) * 128)
        return lax.dot_general(am[b, :, where], bs[b, :, where], nt, preferred_element_type=F32)

    def filled(b, total, tile):
        total = total.reshape(5, NX, 2, 8, 256)[..., tile * 128 : (tile + 1) * 128]
        rows = slice(tile * 8, tile * 8 + 8)
        return jnp.where(maskv[b, :, rows][None] > 0.5, total[:, :, 0] + total[:, :, 1], stv[b, :, :, rows])

    places(0)
    arrived(list_copies)
    places(1)
    places(2)
    onward = []

    def pass_on(i):
        rows = slice(PARTS[i].start * 8, PARTS[i].stop * 8)
        for off in range(PARTS[i].start, PARTS[i].stop):
            if off:
                by_source[off].wait_recv()
        onward.append(beside(irecv.at[0, rows], [irecv.at[1, rows], irecv.at[2, rows]], 2 + i))

    pass_on(0)
    pass_on(1)
    spread(0, NEAR)
    near = collect(0, NEAR)
    pass_on(2)
    spread(0, FAR)
    total = near + collect(0, FAR)
    for tile in range(2):
        fil[:, :, tile * 8 : tile * 8 + 8] = filled(0, total, tile)
    halos = {
        name: (
            pltpu.make_async_remote_copy(
                src_ref=src, dst_ref=dst, send_sem=hs_sem.at[i], recv_sem=hr_sem.at[i], device_id=where, device_id_type=MESH
            ),
            sends,
            receives,
        )
        for i, (name, src, dst, where, sends, receives) in enumerate(
            (
                ("yl", fil.at[:, :, 13:16, :], yl.at[:, :, 5:8, :], {"gy": above}, has_above, has_below),
                ("yr", fil.at[:, :, 0:3, :], yr.at[:, :, 0:3, :], {"gy": below}, has_below, has_above),
            )
        )
    }
    for copy, sends, _ in halos.values():
        pl.when(sends)(copy.start)

    u = [fil[v] for v in range(5)]
    rinv, p = inverse_pressure(u)
    for v, pair in enumerate(split(u, rinv, p, 2, lf[2])):
        for s in range(2):
            fz[s, v * NX : (v + 1) * NX] = pair[s]
    for v, pair in enumerate(split(u, rinv, p, 1, lf[1])):
        for s in range(2):
            for i in range(NX):
                fy[pl.ds((s * 32 + 8) * 16 + v * NX + i, 16, 16), :] = pair[s][i]
    for v, pair in enumerate(split(u, rinv, p, 0, lf[0])):
        for s in range(2):
            fx[s, v, 3:6] = pair[s]

    def along_z(n):
        chg[n] = z_change(fz[0, n], fz[1, n])

    loop(15, along_z)

    for side in (1, 2):
        arrived([onward[0][side - 1], onward[1][side - 1]])
        spread(side, NEAR)
        part[side - 1] = collect(side, NEAR)
    arrived(halos.values())
    for edge, ref, row, base in ((~has_below, yl, 0, 0), (~has_above, yr, 15, 24)):
        u = [jnp.where(edge, fil[v, :, row : row + 1, :], ref[v]) for v in range(5)]
        rinv, p = inverse_pressure(u)
        for v, pair in enumerate(split(u, rinv, p, 1, lf[1])):
            for s in range(2):
                for i in range(NX):
                    fy[pl.ds((s * 32 + base) * 16 + v * NX + i, 8, 16), :] = pair[s][i]

    def along_y(n):
        b, h = n // 2, n % 2

        def window(s, start, count):
            return jnp.stack([fy[pl.ds(pl.multiple_of((s * 32 + start + q) * 16 + h * 8, 8), 8), :] for q in range(count)])

        flux = upwind(*betas(window(0, 5 + 3 * b, 7))) + downwind(*betas(window(1, 6 + 3 * b, 7)))
        for q in range(3):
            fluxy[pl.ds(pl.multiple_of((3 * b + q) * 16 + h * 8, 8), 8), :] = flux[q]

    loop(12, along_y)
    for n in range(15):
        chg[n] = chg[n] + (fluxy[pl.ds(16 + n, 16, 16), :] - fluxy[pl.ds(n, 16, 16), :])

    arrived(raw_copies)
    for side, edge, row, base in ((1, ~has_left, 0, 0), (2, ~has_right, 2, 6)):
        arrived([onward[2][side - 1]])
        spread(side, FAR)
        total = part[side - 1] + collect(side, FAR)
        for tile in range(2):
            rows = slice(tile * 8, tile * 8 + 8)
            brick = filled(side, total, tile)
            u = [jnp.where(edge, fil[v, row : row + 1, rows], brick[v]) for v in range(5)]
            rinv, p = inverse_pressure(u)
            for v, pair in enumerate(split(u, rinv, p, 0, lf[0])):
                for s in range(2):
                    fx[s, v, base : base + 3, rows] = pair[s]
    def along_x(n):
        v, h = n // 2, n % 2
        rows = pl.ds(pl.multiple_of(h * 8, 8), 8)
        flux = upwind(*betas(fx[0, v, 0:8, rows])) + downwind(*betas(fx[1, v, 1:9, rows]))
        change = flux[1:] - flux[:-1] + chg[pl.ds(v * NX, NX), rows]
        mine = fil[v, :, rows]
        out[v, :, rows] = jnp.where(maskv[0, :, rows] > 0.5, mine, mine - (0.125 / 6.0) * change)

    loop(10, along_x)
    for copy in [*frac_copies.values(), *image_copies.values()]:
        copy.wait_send()
    for copy, sends, _ in [*halos.values(), *list_copies, *raw_copies, *onward[0], *onward[1], *onward[2]]:
        pl.when(sends)(copy.wait_send)


def solution(mesh):
    n_gx, n_gy = mesh.shape["gx"], mesh.shape["gy"]

    def on_device(state, lf_speed, ghost_cell, ghost_frac, donor_block):
        hbm = pl.BlockSpec(memory_space=pltpu.HBM)
        vmem = pltpu.VMEM
        dma = pltpu.SemaphoreType.DMA
        brick = (5, NX, NY, NZ)
        return pl.pallas_call(
            functools.partial(kernel, n_gx, n_gy),
            out_shape=jax.ShapeDtypeStruct(brick, F32),
            in_specs=[hbm] * 5,
            out_specs=pl.BlockSpec(memory_space=pltpu.VMEM),
            scratch_shapes=[
                vmem((3,) + brick, F32),
                vmem((16, 192), jnp.int32),
                vmem((3, 16, 192), F32),
                vmem((16, 192), jnp.int32),
                vmem((128, 128), F32),
                vmem((128, 128), F32),
                vmem((128, 128), F32),
                vmem((3, 128, 128), F32),
                vmem((ROWS, 128), jnp.int32),
                vmem((3, ROWS, 128), jnp.int32),
                vmem((240, 256), BF16),
                vmem((ROWS, 4, 5, NY, 128), F32),
                vmem((3, 256, ROWS * 128), BF16),
                vmem((3, 48, ROWS * 128), BF16),
                vmem((3, 240, ROWS * 128), BF16),
                vmem((3, NX, NY, NZ), F32),
                vmem((2, 240, 256), F32),
                vmem(brick, F32),
                vmem((5, NX, 8, NZ), F32),
                vmem((5, NX, 8, NZ), F32),
                vmem((2, 5, 9, NY, NZ), F32),
                vmem((2 * 32 * 16, NZ), F32),
                vmem((2, 15, NY, NZ), F32),
                vmem((18 * 16, NZ), F32),
                vmem((15, NY, NZ), F32),
                pltpu.SMEM((3,), F32),
                dma((5,)),
                dma((n_gy - 1,)),
                dma((n_gy - 1,)),
                dma((n_gy - 1,)),
                dma((n_gy - 1,)),
                dma((2,)),
                dma((2,)),
                dma((10,)),
                dma((10,)),
            ],
            compiler_params=pltpu.CompilerParams(
                collective_id=0, has_side_effects=True, vmem_limit_bytes=40 * 1024 * 1024
            ),
        )(
            *(
                pltpu.with_memory_space_constraint(x, pltpu.HBM)
                for x in (
                    lf_speed,
                    state,
                    ghost_cell.reshape(ghost_cell.shape[2:]),
                    ghost_frac.reshape((3,) + ghost_frac.shape[3:]),
                    donor_block.reshape(donor_block.shape[2:]),
                )
            )
        )

    return jax.shard_map(
        on_device,
        mesh=mesh,
        in_specs=(
            P(None, "gx", "gy", None),
            P(),
            P("gx", "gy", None, None),
            P(None, "gx", "gy", None, None),
            P("gx", "gy", None, None),
        ),
        out_specs=P(None, "gx", "gy", None),
        check_vma=False,
    )
```

```python
import functools

import jax
import jax.numpy as jnp
from jax import lax
from jax.experimental import pallas as pl
from jax.experimental.pallas import tpu as pltpu
from jax.sharding import PartitionSpec as P

MESH = pl.DeviceIdType.MESH
F32 = jnp.float32
BF16 = jnp.bfloat16
SIGN = (1.0, -1.0, -1.0, -1.0, 1.0)
EPS = 16.0e-6
C13 = 13.0 / 3.0
NX, NY, NZ = 3, 16, 128
ROWS = 24


def loop(count, body):
    def step(i, carry):
        body(i)
        return carry

    lax.fori_loop(0, count, step, 0, unroll=True)


def sq(x):
    return x * x


def rcp(x):
    r = pl.reciprocal(x, approx=True)
    return r * (2.0 - x * r)


def iota(shape, dim):
    return lax.broadcasted_iota(jnp.int32, shape, dim)


def betas(w):
    n = w.shape[0] - 4
    d = w[1:] - w[:-1]
    dd = d[1:] - d[:-1]
    e = (C13 * dd) * dd + EPS
    t = dd[1:] - dd[:-1]
    left = e[:n] + sq(3.0 * d[1 : n + 1] - d[:n])
    mid = e[1 : n + 1] + sq(d[1 : n + 1] + d[2 : n + 2])
    right = e[2 : n + 2] + sq(3.0 * d[2 : n + 2] - d[3 : n + 3])
    return w[2 : n + 2], d[1 : n + 1], d[2 : n + 2], t[:n], t[1:], left, mid, right


def upwind(f, dm, dp, tm, tp, left, mid, right):
    a, b, c = sq(mid * right), sq(left * right), 3.0 * sq(left * mid)
    return 6.0 * f + dm + 2.0 * dp - (2.0 * a * tm + c * tp) * rcp(a + 6.0 * b + c)


def downwind(f, dm, dp, tm, tp, left, mid, right):
    a, b, c = sq(mid * left), sq(left * right), 3.0 * sq(mid * right)
    return 6.0 * f - dp - 2.0 * dm + (2.0 * a * tp + c * tm) * rcp(a + 6.0 * b + c)


def z_change(fp, fm):
    lane = iota(fp.shape, 1)
    first, last = lane == 0, lane == NZ - 1
    down = lambda x: pltpu.roll(x, 1, 1)
    up = lambda x: pltpu.roll(x, NZ - 1, 1)

    def parts(f):
        dp = jnp.where(last, 0.0, up(f) - f)
        dm = down(dp)
        dd = dp - dm
        e = (C13 * dd) * dd + EPS
        left, right = e + sq(3.0 * dp - dm), e + sq(3.0 * dm - dp)
        mid = e + sq(dp + dm)
        tm = dd - jnp.where(first, 0.0, down(dd))
        tp = jnp.where(last, 0.0, up(dd)) - dd
        args = (f, dm, dp, tm, tp, jnp.where(first, EPS, down(left)), mid, jnp.where(last, EPS, up(right)))
        return args, dd, left, right

    plus, dd_plus, _, right = parts(fp)
    minus, dd_minus, left, _ = parts(fm)
    rp, rm = upwind(*plus), downwind(*minus)
    f = jnp.where(first, fp, fm)
    dd = jnp.where(first, dd_plus, dd_minus)
    far = jnp.where(first, right, left)
    edge = 6.0 * f - 3.0 * EPS * EPS * dd * rcp(7.0 * sq(far) + 3.0 * EPS * EPS)
    return rp - jnp.where(first, edge, down(rp)) + jnp.where(last, edge, up(rm)) - rm


def inverse_pressure(u):
    rinv = 1.0 / u[0]
    kinetic = (u[1] * u[1] + u[2] * u[2] + u[3] * u[3]) * rinv
    return rinv, 0.4 * (u[4] - 0.5 * kinetic)


def split(u, rinv, p, direction, speed):
    normal = u[1 + direction] * rinv
    result = []
    for v in range(5):
        if v == 0:
            f = u[1 + direction]
        elif v == 4:
            f = normal * (u[4] + p)
        else:
            f = normal * u[v]
            if v == 1 + direction:
                f = f + p
        s = speed * u[v]
        result.append((f + s, f - s))
    return result


OTHER = [8, 15, 14, 13, 12, 11, 10, 9]
NEAR = [0, 1, 2, 3, 4, 5, 6, 10, 11, 12, 13, 14, 15, 16 + 1, 16 + 2, 16 + 3, 16 + 4, 16 + 5, 16 + 6]
FAR = [7, 8, 9, 16 + 7, 16 + 0]
ORDER = NEAR + FAR
PLACE = {row: place for place, row in enumerate(ORDER)}
PARTS = (slice(0, 7), slice(10, 16), slice(7, 10))


def kernel(
    n_gx, n_gy, lf_h, state_h, cell_h, frac_h, donor_h, out,
    stv, cellv, fracv, donv, fsend, frecv, isend, irecv, kq, cq, ss, pp, bs, ohs, am, maskv,
    fil, yl, yr, fx, fy, fz, fluxy, chg, lf,
    in_sem, fs_sem, fr_sem, is_sem, ir_sem, hs_sem, hr_sem, xs_sem, xr_sem, here_sem,
):
    gx, gy = lax.axis_index("gx"), lax.axis_index("gy")
    right, left, above, below = gx + 1, gx - 1, gy + 1, gy - 1
    has_left, has_right, has_below, has_above = gx > 0, gx < n_gx - 1, gy > 0, gy < n_gy - 1
    half = iota((1, 128), 1) < 64
    even = lax.rem(gx, 2) == 0

    loads = [
        pltpu.make_async_copy(src, dst, in_sem.at[i])
        for i, (src, dst) in enumerate(
            ((frac_h, fracv), (donor_h, donv), (state_h, stv.at[0]), (cell_h, cellv), (lf_h, lf))
        )
    ]
    for load in loads:
        load.start()

    def partner(off):
        return lax.rem(gy + off, n_gy)

    barrier = pltpu.get_barrier_semaphore()
    for off in sorted(range(1, n_gy), key=lambda off: -min(off, n_gy - off)):
        pl.semaphore_signal(barrier, inc=1, device_id={"gy": partner(off)}, device_id_type=MESH)
    for inside, other in ((has_left, left), (has_right, right)):

        @pl.when(inside & even)
        def _():
            pl.semaphore_signal(barrier, inc=1, device_id={"gx": other}, device_id_type=MESH)

    def turn(x):
        return pltpu.roll(x, 64, x.ndim - 1)

    def share(tails):
        low = [jnp.where(half, a, turn(b)) for a, b in zip(tails[0::2], tails[1::2])]
        high = [jnp.where(half, turn(a), b) for a, b in zip(tails[0::2], tails[1::2])]
        return low + [tails[-1]], high + [turn(tails[-1])]

    def unshare(low, high):
        rows = []
        for a, b in zip(low, high):
            rows += [jnp.where(half, a, turn(b)), jnp.where(half, turn(a), b)]
        return rows[:-1]

    def by_distance(ref, *lead):
        rows = jnp.concatenate([ref[(*lead, pl.ds(partner(off), 1))] for off in range(16)], axis=0)
        tail = rows[:, 128:192]
        high = jnp.concatenate([tail[off : off + 1] for off in OTHER], axis=0)
        return rows[:, 0:128], jnp.concatenate([tail[0:8], high], axis=1)

    loads[0].wait()
    fsend[...] = jnp.zeros_like(fsend)
    tails = []
    for c in range(3):
        main, tail = by_distance(fracv, c)
        fsend[pl.ds(c, 16, 8), :] = main
        tails.append(tail)
    low, high = share(tails)
    for c in range(2):
        fsend[pl.ds(3 + c, 8, 8), :] = low[c]
        for t, off in enumerate(OTHER):
            fsend[off * 8 + 3 + c : off * 8 + 4 + c, :] = high[c][t : t + 1]
    beside_me = has_left.astype(jnp.int32) + has_right.astype(jnp.int32)
    pl.semaphore_wait(barrier, n_gy - 1 + jnp.where(even, 0, beside_me))

    def message(send, recv, off, s_sem, r_sem):
        copy = pltpu.make_async_remote_copy(
            src_ref=send.at[pl.ds(off * 8, 8), :],
            dst_ref=recv.at[pl.ds((n_gy - off) * 8, 8), :],
            send_sem=s_sem.at[off - 1],
            recv_sem=r_sem.at[n_gy - off - 1],
            device_id={"gy": partner(off)},
            device_id_type=MESH,
        )
        copy.start()
        return copy

    def from_source(copies):
        return {n_gy - off: copy for off, copy in copies.items()}

    offs = [off for t in (0, 7, 6, 5, 4, 3, 2, 1) for off in (OTHER[t], t) if off]
    frac_copies = {off: message(fsend, frecv, off, fs_sem, fr_sem) for off in offs}
    frecv[0:8] = fsend[0:8]

    def beside(src, dsts, i):
        return [
            pltpu.make_async_remote_copy(
                src_ref=src,
                dst_ref=dsts[side],
                send_sem=xs_sem.at[2 * i + side],
                recv_sem=xr_sem.at[2 * i + side],
                device_id={"gx": other},
                device_id_type=MESH,
            )
            for side, other in enumerate((right, left))
        ]

    for inside, other, side in ((has_left, left, 1), (has_right, right, 0)):

        @pl.when(inside & ~even)
        def _():
            pl.semaphore_signal(here_sem.at[side], inc=1, device_id={"gx": other}, device_id_type=MESH)

    loads[3].wait()
    loads[2].wait()
    main, tail = by_distance(cellv)
    packed = jnp.concatenate([main, tail], axis=0)
    cq[0] = jnp.where(packed < 0, -4096, packed)
    loads[1].wait()
    main, tail = by_distance(donv)
    kq[...] = jnp.concatenate([main, tail], axis=0)
    flat = stv[0].reshape(240, 128)
    high = flat.astype(BF16)
    ss[:, 0:128] = high
    ss[:, 128:256] = (flat - high.astype(F32)).astype(BF16)

    def corners(r):
        donor = kq[pl.ds(r, 1), :]
        k = jnp.bitwise_and(donor, 127)
        i0 = jnp.right_shift(donor, 11)
        at = iota((128, 128), 0) - k
        here = jnp.where(at == 0, 1.0, 0.0).astype(F32)
        step = jnp.where(at == 1, 1.0, -here)
        here, step = here.astype(BF16), step.astype(BF16)
        z = jnp.concatenate(
            [jnp.concatenate([here, here], axis=0), jnp.concatenate([step, step], axis=0)], axis=1
        )
        t = jnp.dot(ss[...], z, preferred_element_type=F32)
        for c in range(2):
            tc = t[:, c * 128 : (c + 1) * 128].reshape(5, NX, NY, 128)
            x0 = jnp.where(i0 == 0, tc[:, 0], tc[:, 1])
            x1 = jnp.where(i0 == 0, tc[:, 1], tc[:, 2])
            pp[r, 2 * c] = x0
            pp[r, 2 * c + 1] = x1 - x0

    loop(ROWS, corners)

    def image(r, f0, f1, f2):
        donor = kq[r : r + 1, :]
        j0 = jnp.bitwise_and(jnp.right_shift(donor, 7), 15)
        at = iota((NY, 128), 0) - j0
        wy = jnp.where(at == 0, 1.0 - f1, jnp.where(at == 1, f1, 0.0))
        value = pp[r, 0] + f0 * pp[r, 1] + f2 * (pp[r, 2] + f0 * pp[r, 3])
        return jnp.sum(value * wy, axis=1)

    def row_of(ref, off, c):
        return ref[off * 8 + c : off * 8 + c + 1, :]

    sources = from_source(frac_copies)
    image_copies = {}
    for t in (1, 2, 3, 4, 5, 6, 7, 0):
        both = (OTHER[t], t)
        for off in both:
            if off:
                sources[off].wait_recv()
        for off in both:
            isend[off * 8 : off * 8 + 5, :] = image(off, *(row_of(frecv, off, c) for c in range(3)))
        fracs = unshare(*([row_of(frecv, off, 3 + c) for c in range(2)] for off in (t, OTHER[t])))
        value = image(16 + t, *fracs)
        low, high = share([value[v : v + 1] for v in range(5)])
        for c in range(3):
            isend[t * 8 + 5 + c : t * 8 + 6 + c, :] = low[c]
            isend[OTHER[t] * 8 + 5 + c : OTHER[t] * 8 + 6 + c, :] = high[c]
        for off in both:
            if off:
                image_copies[off] = message(isend, irecv.at[0], off, is_sem, ir_sem)
    irecv[0, 0:8] = isend[0:8]
    by_source = from_source(image_copies)

    loads[4].wait()
    nt = (((1,), (1,)), ((), ()))

    def places(b):
        for row in range(ROWS):
            where = slice(PLACE[row] * 128, PLACE[row] * 128 + 128)
            cell = cq[b, row : row + 1, :]
            j = jnp.right_shift(cell, 7)
            column = jnp.bitwise_or(jnp.bitwise_and(jnp.right_shift(cell, 3), 128), jnp.bitwise_and(cell, 127))
            line = jnp.bitwise_or(jnp.left_shift(jnp.right_shift(cell, 11), 3), jnp.bitwise_and(j, 7))
            bs[b, :, where] = jnp.where(iota((256, 128), 0) == column, 1.0, 0.0).astype(BF16)
            i48 = iota((48, 128), 0)
            want = jnp.bitwise_or(jnp.left_shift(jnp.right_shift(i48, 4), 3), jnp.bitwise_and(i48, 7))
            ohs[b, :, where] = jnp.where(want == line, 1.0, 0.0).astype(BF16)
        count = lax.dot_general(ohs[b], bs[b], nt, preferred_element_type=F32).reshape(NX, 2, 8, 256)
        maskv[b, :, 0:8] = count[:, 0, :, 0:128]
        maskv[b, :, 8:16] = count[:, 0, :, 128:256]

    def spread(b, rows):
        for row in rows:
            where = slice(PLACE[row] * 128, PLACE[row] * 128 + 128)
            if row < 16:
                ghost = [irecv[b, row * 8 + v : row * 8 + v + 1, :] for v in range(5)]
            else:
                ends = (row - 16, OTHER[row - 16])
                low, high = ([irecv[b, a * 8 + 5 + c : a * 8 + 6 + c, :] for c in range(3)] for a in ends)
                ghost = unshare(low, high)
            lines = ohs[b, :, where].reshape(NX, 16, 128)
            for v in range(5):
                g = jnp.broadcast_to(SIGN[v] * ghost[v], (8, 128))
                hi = g.astype(BF16)
                lo = (g - hi.astype(F32)).astype(BF16)
                both = jnp.concatenate([hi, lo], axis=0)
                am[b, v * 48 : (v + 1) * 48, where] = (lines * both[None]).reshape(48, 128)

    def collect(b, rows):
        where = slice(PLACE[rows[0]] * 128, (PLACE[rows[-1]] + 1) * 128)
        return lax.dot_general(am[b, :, where], bs[b, :, where], nt, preferred_element_type=F32)

    def filled(b, total, tile):
        total = total.reshape(5, NX, 2, 8, 256)[..., tile * 128 : (tile + 1) * 128]
        rows = slice(tile * 8, tile * 8 + 8)
        return jnp.where(maskv[b, :, rows][None] > 0.5, total[:, :, 0] + total[:, :, 1], stv[b, :, :, rows])

    list_copies = beside(cq.at[0], [cq.at[1], cq.at[2]], 0)
    raw_copies = beside(stv.at[0], [stv.at[1], stv.at[2]], 1)
    slices = [slice(part.start * 8, part.stop * 8) for part in PARTS]
    passed = [beside(irecv.at[0, rows], [irecv.at[1, rows], irecv.at[2, rows]], 2 + i) for i, rows in enumerate(slices)]
    side_copies = [list_copies, raw_copies] + passed

    near_left = has_left & (lax.rem(gx, 8) != 0)
    far_left = has_left & (lax.rem(gx, 8) == 0)

    def start(copies):
        pl.when(has_right)(copies[0].start)
        pl.when(near_left)(copies[1].start)

    def arrived(copies, side):
        pl.when((has_left, has_right)[side])(copies[side].wait_recv)

    def answered(side, expected):
        @pl.when(expected & even)
        def _():
            pl.semaphore_wait(here_sem.at[side], 1)

    answered(0, near_left)
    answered(1, has_right)
    start(list_copies)
    start(raw_copies)
    places(0)
    for i, part in enumerate(PARTS):
        for off in range(part.start, part.stop):
            if off:
                by_source[off].wait_recv()
        start(passed[i])
    spread(0, ORDER)
    total = collect(0, ORDER)
    for tile in range(2):
        fil[:, :, tile * 8 : tile * 8 + 8] = filled(0, total, tile)
    halos = {
        name: (
            pltpu.make_async_remote_copy(
                src_ref=src, dst_ref=dst, send_sem=hs_sem.at[i], recv_sem=hr_sem.at[i], device_id=where, device_id_type=MESH
            ),
            sends,
            receives,
        )
        for i, (name, src, dst, where, sends, receives) in enumerate(
            (
                ("yl", fil.at[:, :, 13:16, :], yl.at[:, :, 5:8, :], {"gy": above}, has_above, has_below),
                ("yr", fil.at[:, :, 0:3, :], yr.at[:, :, 0:3, :], {"gy": below}, has_below, has_above),
            )
        )
    }
    for copy, sends, _ in halos.values():
        pl.when(sends)(copy.start)

    u = [fil[v] for v in range(5)]
    rinv, p = inverse_pressure(u)
    for v, pair in enumerate(split(u, rinv, p, 2, lf[2])):
        for s in range(2):
            fz[s, v * NX : (v + 1) * NX] = pair[s]
    for v, pair in enumerate(split(u, rinv, p, 1, lf[1])):
        for s in range(2):
            for i in range(NX):
                fy[pl.ds((s * 32 + 8) * 16 + v * NX + i, 16, 16), :] = pair[s][i]
    for v, pair in enumerate(split(u, rinv, p, 0, lf[0])):
        for s in range(2):
            fx[s, v, 3:6] = pair[s]

    def along_z(n):
        chg[n] = z_change(fz[0, n], fz[1, n])

    loop(15, along_z)

    for copy, _, receives in halos.values():
        pl.when(receives)(copy.wait_recv)
    for edge, ref, row, base in ((~has_below, yl, 0, 0), (~has_above, yr, 15, 24)):
        u = [jnp.where(edge, fil[v, :, row : row + 1, :], ref[v]) for v in range(5)]
        rinv, p = inverse_pressure(u)
        for v, pair in enumerate(split(u, rinv, p, 1, lf[1])):
            for s in range(2):
                for i in range(NX):
                    fy[pl.ds((s * 32 + base) * 16 + v * NX + i, 8, 16), :] = pair[s][i]

    def along_y(n):
        b, h = n // 2, n % 2

        def window(s, start, count):
            return jnp.stack([fy[pl.ds(pl.multiple_of((s * 32 + start + q) * 16 + h * 8, 8), 8), :] for q in range(count)])

        flux = upwind(*betas(window(0, 5 + 3 * b, 7))) + downwind(*betas(window(1, 6 + 3 * b, 7)))
        for q in range(3):
            fluxy[pl.ds(pl.multiple_of((3 * b + q) * 16 + h * 8, 8), 8), :] = flux[q]

    loop(12, along_y)
    for n in range(15):
        chg[n] = chg[n] + (fluxy[pl.ds(16 + n, 16, 16), :] - fluxy[pl.ds(n, 16, 16), :])

    answered(0, far_left)
    for copies in side_copies:
        pl.when(far_left)(copies[1].start)
    for side, edge, row, base in ((2, ~has_right, 2, 6), (1, ~has_left, 0, 0)):
        arrived(list_copies, side - 1)
        places(side)
        for copies in (raw_copies, passed[0], passed[1]):
            arrived(copies, side - 1)
        spread(side, NEAR)
        total = collect(side, NEAR)
        arrived(passed[2], side - 1)
        spread(side, FAR)
        total = total + collect(side, FAR)
        for tile in range(2):
            rows = slice(tile * 8, tile * 8 + 8)
            brick = filled(side, total, tile)
            u = [jnp.where(edge, fil[v, row : row + 1, rows], brick[v]) for v in range(5)]
            rinv, p = inverse_pressure(u)
            for v, pair in enumerate(split(u, rinv, p, 0, lf[0])):
                for s in range(2):
                    fx[s, v, base : base + 3, rows] = pair[s]
    def along_x(n):
        v, h = n // 2, n % 2
        rows = pl.ds(pl.multiple_of(h * 8, 8), 8)
        flux = upwind(*betas(fx[0, v, 0:8, rows])) + downwind(*betas(fx[1, v, 1:9, rows]))
        change = flux[1:] - flux[:-1] + chg[pl.ds(v * NX, NX), rows]
        mine = fil[v, :, rows]
        out[v, :, rows] = jnp.where(maskv[0, :, rows] > 0.5, mine, mine - (0.125 / 6.0) * change)

    loop(10, along_x)
    for copy in [*frac_copies.values(), *image_copies.values()]:
        copy.wait_send()
    for copy, sends, _ in halos.values():
        pl.when(sends)(copy.wait_send)
    for copies in side_copies:
        pl.when(has_right)(copies[0].wait_send)
        pl.when(has_left)(copies[1].wait_send)


def solution(mesh):
    n_gx, n_gy = mesh.shape["gx"], mesh.shape["gy"]

    def on_device(state, lf_speed, ghost_cell, ghost_frac, donor_block):
        hbm = pl.BlockSpec(memory_space=pltpu.HBM)
        vmem = pltpu.VMEM
        dma = pltpu.SemaphoreType.DMA
        brick = (5, NX, NY, NZ)
        return pl.pallas_call(
            functools.partial(kernel, n_gx, n_gy),
            out_shape=jax.ShapeDtypeStruct(brick, F32),
            in_specs=[hbm] * 5,
            out_specs=pl.BlockSpec(memory_space=pltpu.VMEM),
            scratch_shapes=[
                vmem((3,) + brick, F32),
                vmem((16, 192), jnp.int32),
                vmem((3, 16, 192), F32),
                vmem((16, 192), jnp.int32),
                vmem((128, 128), F32),
                vmem((128, 128), F32),
                vmem((128, 128), F32),
                vmem((3, 128, 128), F32),
                vmem((ROWS, 128), jnp.int32),
                vmem((3, ROWS, 128), jnp.int32),
                vmem((240, 256), BF16),
                vmem((ROWS, 4, 5, NY, 128), F32),
                vmem((3, 256, ROWS * 128), BF16),
                vmem((3, 48, ROWS * 128), BF16),
                vmem((3, 240, ROWS * 128), BF16),
                vmem((3, NX, NY, NZ), F32),
                vmem(brick, F32),
                vmem((5, NX, 8, NZ), F32),
                vmem((5, NX, 8, NZ), F32),
                vmem((2, 5, 9, NY, NZ), F32),
                vmem((2 * 32 * 16, NZ), F32),
                vmem((2, 15, NY, NZ), F32),
                vmem((18 * 16, NZ), F32),
                vmem((15, NY, NZ), F32),
                pltpu.SMEM((3,), F32),
                dma((5,)),
                dma((n_gy - 1,)),
                dma((n_gy - 1,)),
                dma((n_gy - 1,)),
                dma((n_gy - 1,)),
                dma((2,)),
                dma((2,)),
                dma((10,)),
                dma((10,)),
                pltpu.SemaphoreType.REGULAR((2,)),
            ],
            compiler_params=pltpu.CompilerParams(
                collective_id=0, has_side_effects=True, vmem_limit_bytes=40 * 1024 * 1024
            ),
        )(
            *(
                pltpu.with_memory_space_constraint(x, pltpu.HBM)
                for x in (
                    lf_speed,
                    state,
                    ghost_cell.reshape(ghost_cell.shape[2:]),
                    ghost_frac.reshape((3,) + ghost_frac.shape[3:]),
                    donor_block.reshape(donor_block.shape[2:]),
                )
            )
        )

    return jax.shard_map(
        on_device,
        mesh=mesh,
        in_specs=(
            P(None, "gx", "gy", None),
            P(),
            P("gx", "gy", None, None),
            P(None, "gx", "gy", None, None),
            P("gx", "gy", None, None),
        ),
        out_specs=P(None, "gx", "gy", None),
        check_vma=False,
    )
```

```python
import functools

import jax
import jax.numpy as jnp
from jax import lax
from jax.experimental import pallas as pl
from jax.experimental.pallas import tpu as pltpu
from jax.sharding import PartitionSpec as P

MESH = pl.DeviceIdType.MESH
F32 = jnp.float32
BF16 = jnp.bfloat16
SIGN = (1.0, -1.0, -1.0, -1.0, 1.0)
EPS = 16.0e-6
C13 = 13.0 / 3.0
NX, NY, NZ = 3, 16, 128
ROWS = 24


def loop(count, body):
    def step(i, carry):
        body(i)
        return carry

    lax.fori_loop(0, count, step, 0, unroll=True)


def sq(x):
    return x * x


def rcp(x):
    r = pl.reciprocal(x, approx=True)
    return r * (2.0 - x * r)


def iota(shape, dim):
    return lax.broadcasted_iota(jnp.int32, shape, dim)


def betas(w):
    n = w.shape[0] - 4
    d = w[1:] - w[:-1]
    dd = d[1:] - d[:-1]
    e = (C13 * dd) * dd + EPS
    t = dd[1:] - dd[:-1]
    left = e[:n] + sq(3.0 * d[1 : n + 1] - d[:n])
    mid = e[1 : n + 1] + sq(d[1 : n + 1] + d[2 : n + 2])
    right = e[2 : n + 2] + sq(3.0 * d[2 : n + 2] - d[3 : n + 3])
    return w[2 : n + 2], d[1 : n + 1], d[2 : n + 2], t[:n], t[1:], left, mid, right


def upwind(f, dm, dp, tm, tp, left, mid, right):
    a, b, c = sq(mid * right), sq(left * right), 3.0 * sq(left * mid)
    return 6.0 * f + dm + 2.0 * dp - (2.0 * a * tm + c * tp) * rcp(a + 6.0 * b + c)


def downwind(f, dm, dp, tm, tp, left, mid, right):
    a, b, c = sq(mid * left), sq(left * right), 3.0 * sq(mid * right)
    return 6.0 * f - dp - 2.0 * dm + (2.0 * a * tp + c * tm) * rcp(a + 6.0 * b + c)


def z_change(fp, fm):
    lane = iota(fp.shape, 1)
    first, last = lane == 0, lane == NZ - 1
    down = lambda x: pltpu.roll(x, 1, 1)
    up = lambda x: pltpu.roll(x, NZ - 1, 1)

    def parts(f):
        dp = jnp.where(last, 0.0, up(f) - f)
        dm = down(dp)
        dd = dp - dm
        e = (C13 * dd) * dd + EPS
        left, right = e + sq(3.0 * dp - dm), e + sq(3.0 * dm - dp)
        mid = e + sq(dp + dm)
        tm = dd - jnp.where(first, 0.0, down(dd))
        tp = jnp.where(last, 0.0, up(dd)) - dd
        args = (f, dm, dp, tm, tp, jnp.where(first, EPS, down(left)), mid, jnp.where(last, EPS, up(right)))
        return args, dd, left, right

    plus, dd_plus, _, right = parts(fp)
    minus, dd_minus, left, _ = parts(fm)
    rp, rm = upwind(*plus), downwind(*minus)
    f = jnp.where(first, fp, fm)
    dd = jnp.where(first, dd_plus, dd_minus)
    far = jnp.where(first, right, left)
    edge = 6.0 * f - 3.0 * EPS * EPS * dd * rcp(7.0 * sq(far) + 3.0 * EPS * EPS)
    return rp - jnp.where(first, edge, down(rp)) + jnp.where(last, edge, up(rm)) - rm


def inverse_pressure(u):
    rinv = 1.0 / u[0]
    kinetic = (u[1] * u[1] + u[2] * u[2] + u[3] * u[3]) * rinv
    return rinv, 0.4 * (u[4] - 0.5 * kinetic)


def split(u, rinv, p, direction, speed):
    normal = u[1 + direction] * rinv
    result = []
    for v in range(5):
        if v == 0:
            f = u[1 + direction]
        elif v == 4:
            f = normal * (u[4] + p)
        else:
            f = normal * u[v]
            if v == 1 + direction:
                f = f + p
        s = speed * u[v]
        result.append((f + s, f - s))
    return result


OTHER = [8, 15, 14, 13, 12, 11, 10, 9]
NEAR = [0, 1, 2, 3, 4, 5, 6, 10, 11, 12, 13, 14, 15, 16 + 1, 16 + 2, 16 + 3, 16 + 4, 16 + 5, 16 + 6]
FAR = [7, 8, 9, 16 + 7, 16 + 0]
ORDER = NEAR + FAR
PLACE = {row: place for place, row in enumerate(ORDER)}
PARTS = (slice(0, 7), slice(10, 16), slice(7, 10))


def kernel(
    n_gx, n_gy, lf_h, state_h, cell_h, frac_h, donor_h, out,
    stv, cellv, fracv, donv, fsend, frecv, isend, irecv, kq, cq, ss, pp, bs, ohs, am, maskv,
    fil, beyond, yl, yr, fx, fy, fz, fluxy, chg, lf,
    in_sem, fs_sem, fr_sem, is_sem, ir_sem, hs_sem, hr_sem, xs_sem, xr_sem, ds_sem, dr_sem, here_sem,
):
    gx, gy = lax.axis_index("gx"), lax.axis_index("gy")
    right, left, above, below = gx + 1, gx - 1, gy + 1, gy - 1
    has_left, has_right, has_below, has_above = gx > 0, gx < n_gx - 1, gy > 0, gy < n_gy - 1
    half = iota((1, 128), 1) < 64
    even = lax.rem(gx, 2) == 0
    near_left = has_left & (lax.rem(gx, 8) != 0)
    far_left = has_left & (lax.rem(gx, 8) == 0)
    far_right = has_right & (lax.rem(gx, 8) == 7)

    def partner(off):
        return lax.rem(gy + off, n_gy)

    barrier = pltpu.get_barrier_semaphore()
    for off in sorted(range(1, n_gy), key=lambda off: -min(off, n_gy - off)):
        pl.semaphore_signal(barrier, inc=1, device_id={"gy": partner(off)}, device_id_type=MESH)
    for inside, other in ((near_left, left), (has_right, right)):

        @pl.when(inside & even)
        def _():
            pl.semaphore_signal(barrier, inc=1, device_id={"gx": other}, device_id_type=MESH)

    @pl.when(far_left)
    def _():
        for off in range(n_gy):
            where = {"gx": left, "gy": partner(off)}
            pl.semaphore_signal(barrier, inc=1, device_id=where, device_id_type=MESH)

    loads = [
        pltpu.make_async_copy(src, dst, in_sem.at[i])
        for i, (src, dst) in enumerate(
            ((frac_h, fracv), (donor_h, donv), (state_h, stv.at[0]), (cell_h, cellv), (lf_h, lf))
        )
    ]
    for load in loads:
        load.start()

    def turn(x):
        return pltpu.roll(x, 64, x.ndim - 1)

    def share(tails):
        low = [jnp.where(half, a, turn(b)) for a, b in zip(tails[0::2], tails[1::2])]
        high = [jnp.where(half, turn(a), b) for a, b in zip(tails[0::2], tails[1::2])]
        return low + [tails[-1]], high + [turn(tails[-1])]

    def unshare(low, high):
        rows = []
        for a, b in zip(low, high):
            rows += [jnp.where(half, a, turn(b)), jnp.where(half, turn(a), b)]
        return rows[:-1]

    def by_distance(ref, *lead):
        rows = jnp.concatenate([ref[(*lead, pl.ds(partner(off), 1))] for off in range(16)], axis=0)
        tail = rows[:, 128:192]
        high = jnp.concatenate([tail[off : off + 1] for off in OTHER], axis=0)
        return rows[:, 0:128], jnp.concatenate([tail[0:8], high], axis=1)

    loads[0].wait()
    fsend[...] = jnp.zeros_like(fsend)
    tails = []
    for c in range(3):
        main, tail = by_distance(fracv, c)
        fsend[pl.ds(c, 16, 8), :] = main
        tails.append(tail)
    low, high = share(tails)
    for c in range(2):
        fsend[pl.ds(3 + c, 8, 8), :] = low[c]
        for t, off in enumerate(OTHER):
            fsend[off * 8 + 3 + c : off * 8 + 4 + c, :] = high[c][t : t + 1]
    beside_me = has_left.astype(jnp.int32) + jnp.where(far_right, n_gy, has_right.astype(jnp.int32))
    pl.semaphore_wait(barrier, n_gy - 1 + jnp.where(even, 0, beside_me))

    def message(send, recv, off, s_sem, r_sem):
        copy = pltpu.make_async_remote_copy(
            src_ref=send.at[pl.ds(off * 8, 8), :],
            dst_ref=recv.at[pl.ds((n_gy - off) * 8, 8), :],
            send_sem=s_sem.at[off - 1],
            recv_sem=r_sem.at[n_gy - off - 1],
            device_id={"gy": partner(off)},
            device_id_type=MESH,
        )
        copy.start()
        return copy

    def from_source(copies):
        return {n_gy - off: copy for off, copy in copies.items()}

    offs = [off for t in (0, 7, 6, 5, 4, 3, 2, 1) for off in (OTHER[t], t) if off]
    frac_copies = {off: message(fsend, frecv, off, fs_sem, fr_sem) for off in offs}
    frecv[0:8] = fsend[0:8]

    def beside(src, dsts, i):
        return [
            pltpu.make_async_remote_copy(
                src_ref=src,
                dst_ref=dsts[side],
                send_sem=xs_sem.at[2 * i + side],
                recv_sem=xr_sem.at[2 * i + side],
                device_id={"gx": other},
                device_id_type=MESH,
            )
            for side, other in enumerate((right, left))
        ]

    for inside, other, side in ((has_left, left, 1), (has_right, right, 0)):

        @pl.when(inside & ~even)
        def _():
            pl.semaphore_signal(here_sem.at[side], inc=1, device_id={"gx": other}, device_id_type=MESH)

    loads[3].wait()
    loads[2].wait()
    main, tail = by_distance(cellv)
    packed = jnp.concatenate([main, tail], axis=0)
    cq[0] = jnp.where(packed < 0, -4096, packed)
    loads[1].wait()
    main, tail = by_distance(donv)
    kq[...] = jnp.concatenate([main, tail], axis=0)
    flat = stv[0].reshape(240, 128)
    high = flat.astype(BF16)
    ss[:, 0:128] = high
    ss[:, 128:256] = (flat - high.astype(F32)).astype(BF16)

    def corners(r):
        donor = kq[pl.ds(r, 1), :]
        k = jnp.bitwise_and(donor, 127)
        i0 = jnp.right_shift(donor, 11)
        at = iota((128, 128), 0) - k
        here = jnp.where(at == 0, 1.0, 0.0).astype(F32)
        step = jnp.where(at == 1, 1.0, -here)
        here, step = here.astype(BF16), step.astype(BF16)
        z = jnp.concatenate(
            [jnp.concatenate([here, here], axis=0), jnp.concatenate([step, step], axis=0)], axis=1
        )
        t = jnp.dot(ss[...], z, preferred_element_type=F32)
        for c in range(2):
            tc = t[:, c * 128 : (c + 1) * 128].reshape(5, NX, NY, 128)
            x0 = jnp.where(i0 == 0, tc[:, 0], tc[:, 1])
            x1 = jnp.where(i0 == 0, tc[:, 1], tc[:, 2])
            pp[r, 2 * c] = x0
            pp[r, 2 * c + 1] = x1 - x0

    loop(ROWS, corners)

    def image(r, f0, f1, f2):
        donor = kq[r : r + 1, :]
        j0 = jnp.bitwise_and(jnp.right_shift(donor, 7), 15)
        at = iota((NY, 128), 0) - j0
        wy = jnp.where(at == 0, 1.0 - f1, jnp.where(at == 1, f1, 0.0))
        value = pp[r, 0] + f0 * pp[r, 1] + f2 * (pp[r, 2] + f0 * pp[r, 3])
        return jnp.sum(value * wy, axis=1)

    def row_of(ref, off, c):
        return ref[off * 8 + c : off * 8 + c + 1, :]

    sources = from_source(frac_copies)
    image_copies = {}
    direct = {
        off: pltpu.make_async_remote_copy(
            src_ref=isend.at[pl.ds(off * 8, 8), :],
            dst_ref=irecv.at[1, pl.ds((n_gy - off) % n_gy * 8, 8), :],
            send_sem=ds_sem.at[off],
            recv_sem=dr_sem.at[(n_gy - off) % n_gy],
            device_id={"gx": right, "gy": partner(off)},
            device_id_type=MESH,
        )
        for off in range(n_gy)
    }
    from_left = {(n_gy - off) % n_gy: copy for off, copy in direct.items()}
    for t in (1, 2, 3, 4, 5, 6, 7, 0):
        both = (OTHER[t], t)
        for off in both:
            if off:
                sources[off].wait_recv()
        for off in both:
            isend[off * 8 : off * 8 + 5, :] = image(off, *(row_of(frecv, off, c) for c in range(3)))
        fracs = unshare(*([row_of(frecv, off, 3 + c) for c in range(2)] for off in (t, OTHER[t])))
        value = image(16 + t, *fracs)
        low, high = share([value[v : v + 1] for v in range(5)])
        for c in range(3):
            isend[t * 8 + 5 + c : t * 8 + 6 + c, :] = low[c]
            isend[OTHER[t] * 8 + 5 + c : OTHER[t] * 8 + 6 + c, :] = high[c]
        for off in both:
            pl.when(far_right)(direct[off].start)
        for off in both:
            if off:
                image_copies[off] = message(isend, irecv.at[0], off, is_sem, ir_sem)
    irecv[0, 0:8] = isend[0:8]
    by_source = from_source(image_copies)

    loads[4].wait()
    nt = (((1,), (1,)), ((), ()))

    def places(b):
        for row in range(ROWS):
            where = slice(PLACE[row] * 128, PLACE[row] * 128 + 128)
            cell = cq[b, row : row + 1, :]
            j = jnp.right_shift(cell, 7)
            column = jnp.bitwise_or(jnp.bitwise_and(jnp.right_shift(cell, 3), 128), jnp.bitwise_and(cell, 127))
            line = jnp.bitwise_or(jnp.left_shift(jnp.right_shift(cell, 11), 3), jnp.bitwise_and(j, 7))
            bs[b, :, where] = jnp.where(iota((256, 128), 0) == column, 1.0, 0.0).astype(BF16)
            i48 = iota((48, 128), 0)
            want = jnp.bitwise_or(jnp.left_shift(jnp.right_shift(i48, 4), 3), jnp.bitwise_and(i48, 7))
            ohs[b, :, where] = jnp.where(want == line, 1.0, 0.0).astype(BF16)
        count = lax.dot_general(ohs[b], bs[b], nt, preferred_element_type=F32).reshape(NX, 2, 8, 256)
        maskv[b, :, 0:8] = count[:, 0, :, 0:128]
        maskv[b, :, 8:16] = count[:, 0, :, 128:256]

    def spread(b, rows):
        for row in rows:
            where = slice(PLACE[row] * 128, PLACE[row] * 128 + 128)
            if row < 16:
                ghost = [irecv[b, row * 8 + v : row * 8 + v + 1, :] for v in range(5)]
            else:
                ends = (row - 16, OTHER[row - 16])
                low, high = ([irecv[b, a * 8 + 5 + c : a * 8 + 6 + c, :] for c in range(3)] for a in ends)
                ghost = unshare(low, high)
            lines = ohs[b, :, where].reshape(NX, 16, 128)
            for v in range(5):
                g = jnp.broadcast_to(SIGN[v] * ghost[v], (8, 128))
                hi = g.astype(BF16)
                lo = (g - hi.astype(F32)).astype(BF16)
                both = jnp.concatenate([hi, lo], axis=0)
                am[b, v * 48 : (v + 1) * 48, where] = (lines * both[None]).reshape(48, 128)

    def collect(b, rows):
        where = slice(PLACE[rows[0]] * 128, (PLACE[rows[-1]] + 1) * 128)
        return lax.dot_general(am[b, :, where], bs[b, :, where], nt, preferred_element_type=F32)

    def filled(b, total, tile):
        total = total.reshape(5, NX, 2, 8, 256)[..., tile * 128 : (tile + 1) * 128]
        rows = slice(tile * 8, tile * 8 + 8)
        return jnp.where(maskv[b, :, rows][None] > 0.5, total[:, :, 0] + total[:, :, 1], stv[b, :, :, rows])

    list_copies = beside(cq.at[0], [cq.at[1], cq.at[2]], 0)
    raw_copies = beside(stv.at[0], [stv.at[1], stv.at[2]], 1)
    slices = [slice(part.start * 8, part.stop * 8) for part in PARTS]
    passed = [beside(irecv.at[0, rows], [irecv.at[1, rows], irecv.at[2, rows]], 2 + i) for i, rows in enumerate(slices)]
    side_copies = [list_copies, raw_copies] + passed

    def start(copies, to_right=has_right):
        pl.when(to_right)(copies[0].start)
        pl.when(near_left)(copies[1].start)

    def arrived(copies, side):
        pl.when((has_left, has_right)[side])(copies[side].wait_recv)

    def answered(side, expected):
        @pl.when(expected & even)
        def _():
            pl.semaphore_wait(here_sem.at[side], 1)

    answered(0, near_left)
    answered(1, has_right)
    start(list_copies)
    start(raw_copies)
    places(0)
    arrived(list_copies, 1)
    places(2)

    @pl.when(near_left)
    def _():
        list_copies[0].wait_recv()
        places(1)

    for i, part in enumerate(PARTS):
        for off in range(part.start, part.stop):
            if off:
                by_source[off].wait_recv()
        start(passed[i], has_right & ~far_right)
    spread(0, ORDER)
    total = collect(0, ORDER)
    for tile in range(2):
        fil[:, :, tile * 8 : tile * 8 + 8] = filled(0, total, tile)
    halos = {
        name: (
            pltpu.make_async_remote_copy(
                src_ref=src, dst_ref=dst, send_sem=hs_sem.at[i], recv_sem=hr_sem.at[i], device_id=where, device_id_type=MESH
            ),
            sends,
            receives,
        )
        for i, (name, src, dst, where, sends, receives) in enumerate(
            (
                ("yl", fil.at[:, :, 13:16, :], yl.at[:, :, 5:8, :], {"gy": above}, has_above, has_below),
                ("yr", fil.at[:, :, 0:3, :], yr.at[:, :, 0:3, :], {"gy": below}, has_below, has_above),
            )
        )
    }
    for copy, sends, _ in halos.values():
        pl.when(sends)(copy.start)

    u = [fil[v] for v in range(5)]
    rinv, p = inverse_pressure(u)
    for v, pair in enumerate(split(u, rinv, p, 2, lf[2])):
        for s in range(2):
            fz[s, v * NX : (v + 1) * NX] = pair[s]
    for v, pair in enumerate(split(u, rinv, p, 1, lf[1])):
        for s in range(2):
            for i in range(NX):
                fy[pl.ds((s * 32 + 8) * 16 + v * NX + i, 16, 16), :] = pair[s][i]
    for v, pair in enumerate(split(u, rinv, p, 0, lf[0])):
        for s in range(2):
            fx[s, v, 3:6] = pair[s]

    def along_z(n):
        chg[n] = z_change(fz[0, n], fz[1, n])

    loop(15, along_z)

    for copy, _, receives in halos.values():
        pl.when(receives)(copy.wait_recv)
    for edge, ref, row, base in ((~has_below, yl, 0, 0), (~has_above, yr, 15, 24)):
        u = [jnp.where(edge, fil[v, :, row : row + 1, :], ref[v]) for v in range(5)]
        rinv, p = inverse_pressure(u)
        for v, pair in enumerate(split(u, rinv, p, 1, lf[1])):
            for s in range(2):
                for i in range(NX):
                    fy[pl.ds((s * 32 + base) * 16 + v * NX + i, 8, 16), :] = pair[s][i]

    def along_y(n):
        b, h = n // 2, n % 2

        def window(s, start, count):
            return jnp.stack([fy[pl.ds(pl.multiple_of((s * 32 + start + q) * 16 + h * 8, 8), 8), :] for q in range(count)])

        flux = upwind(*betas(window(0, 5 + 3 * b, 7))) + downwind(*betas(window(1, 6 + 3 * b, 7)))
        for q in range(3):
            fluxy[pl.ds(pl.multiple_of((3 * b + q) * 16 + h * 8, 8), 8), :] = flux[q]

    loop(12, along_y)
    for n in range(15):
        chg[n] = chg[n] + (fluxy[pl.ds(16 + n, 16, 16), :] - fluxy[pl.ds(n, 16, 16), :])

    answered(0, far_left)
    for copies in side_copies:
        pl.when(far_left)(copies[1].start)
    @pl.when(far_left)
    def _():
        list_copies[0].wait_recv()
        places(1)

    def parts_arrived(side, which):
        for i in which:
            if side == 2:
                arrived(passed[i], 1)
            else:
                pl.when(near_left)(passed[i][0].wait_recv)

                @pl.when(far_left)
                def _():
                    for off in range(PARTS[i].start, PARTS[i].stop):
                        from_left[off].wait_recv()

    for side, inside, row, base in ((2, has_right, 2, 6), (1, has_left, 0, 0)):

        @pl.when(inside)
        def _():
            parts_arrived(side, (0, 1))
            spread(side, NEAR)
            total = collect(side, NEAR)
            parts_arrived(side, (2,))
            spread(side, FAR)
            total = total + collect(side, FAR)
            arrived(raw_copies, side - 1)
            for tile in range(2):
                beyond[:, :, tile * 8 : tile * 8 + 8] = filled(side, total, tile)

        @pl.when(~inside)
        def _():
            for i in range(NX):
                beyond[:, i] = fil[:, row]

        u = [beyond[v] for v in range(5)]
        rinv, p = inverse_pressure(u)
        for v, pair in enumerate(split(u, rinv, p, 0, lf[0])):
            for s in range(2):
                fx[s, v, base : base + 3] = pair[s]

    def along_x(n):
        v, h = n // 2, n % 2
        rows = pl.ds(pl.multiple_of(h * 8, 8), 8)
        flux = upwind(*betas(fx[0, v, 0:8, rows])) + downwind(*betas(fx[1, v, 1:9, rows]))
        change = flux[1:] - flux[:-1] + chg[pl.ds(v * NX, NX), rows]
        mine = fil[v, :, rows]
        out[v, :, rows] = jnp.where(maskv[0, :, rows] > 0.5, mine, mine - (0.125 / 6.0) * change)

    loop(10, along_x)
    for copy in [*frac_copies.values(), *image_copies.values()]:
        copy.wait_send()
    for copy, sends, _ in halos.values():
        pl.when(sends)(copy.wait_send)
    for copies in side_copies:
        to_right = has_right if copies is list_copies or copies is raw_copies else has_right & ~far_right
        pl.when(to_right)(copies[0].wait_send)
        pl.when(has_left)(copies[1].wait_send)
    for copy in direct.values():
        pl.when(far_right)(copy.wait_send)


def solution(mesh):
    n_gx, n_gy = mesh.shape["gx"], mesh.shape["gy"]

    def on_device(state, lf_speed, ghost_cell, ghost_frac, donor_block):
        hbm = pl.BlockSpec(memory_space=pltpu.HBM)
        vmem = pltpu.VMEM
        dma = pltpu.SemaphoreType.DMA
        brick = (5, NX, NY, NZ)
        return pl.pallas_call(
            functools.partial(kernel, n_gx, n_gy),
            out_shape=jax.ShapeDtypeStruct(brick, F32),
            in_specs=[hbm] * 5,
            out_specs=pl.BlockSpec(memory_space=pltpu.VMEM),
            scratch_shapes=[
                vmem((3,) + brick, F32),
                vmem((16, 192), jnp.int32),
                vmem((3, 16, 192), F32),
                vmem((16, 192), jnp.int32),
                vmem((128, 128), F32),
                vmem((128, 128), F32),
                vmem((128, 128), F32),
                vmem((3, 128, 128), F32),
                vmem((ROWS, 128), jnp.int32),
                vmem((3, ROWS, 128), jnp.int32),
                vmem((240, 256), BF16),
                vmem((ROWS, 4, 5, NY, 128), F32),
                vmem((3, 256, ROWS * 128), BF16),
                vmem((3, 48, ROWS * 128), BF16),
                vmem((3, 240, ROWS * 128), BF16),
                vmem((3, NX, NY, NZ), F32),
                vmem(brick, F32),
                vmem(brick, F32),
                vmem((5, NX, 8, NZ), F32),
                vmem((5, NX, 8, NZ), F32),
                vmem((2, 5, 9, NY, NZ), F32),
                vmem((2 * 32 * 16, NZ), F32),
                vmem((2, 15, NY, NZ), F32),
                vmem((18 * 16, NZ), F32),
                vmem((15, NY, NZ), F32),
                pltpu.SMEM((3,), F32),
                dma((5,)),
                dma((n_gy - 1,)),
                dma((n_gy - 1,)),
                dma((n_gy - 1,)),
                dma((n_gy - 1,)),
                dma((2,)),
                dma((2,)),
                dma((10,)),
                dma((10,)),
                dma((n_gy,)),
                dma((n_gy,)),
                pltpu.SemaphoreType.REGULAR((2,)),
            ],
            compiler_params=pltpu.CompilerParams(
                collective_id=0, has_side_effects=True, vmem_limit_bytes=40 * 1024 * 1024
            ),
        )(
            *(
                pltpu.with_memory_space_constraint(x, pltpu.HBM)
                for x in (
                    lf_speed,
                    state,
                    ghost_cell.reshape(ghost_cell.shape[2:]),
                    ghost_frac.reshape((3,) + ghost_frac.shape[3:]),
                    donor_block.reshape(donor_block.shape[2:]),
                )
            )
        )

    return jax.shard_map(
        on_device,
        mesh=mesh,
        in_specs=(
            P(None, "gx", "gy", None),
            P(),
            P("gx", "gy", None, None),
            P(None, "gx", "gy", None, None),
            P("gx", "gy", None, None),
        ),
        out_specs=P(None, "gx", "gy", None),
        check_vma=False,
    )
```

```python
import functools

import jax
import jax.numpy as jnp
from jax import lax
from jax.experimental import pallas as pl
from jax.experimental.pallas import tpu as pltpu
from jax.sharding import PartitionSpec as P

MESH = pl.DeviceIdType.MESH
F32 = jnp.float32
BF16 = jnp.bfloat16
SIGN = (1.0, -1.0, -1.0, -1.0, 1.0)
EPS = 16.0e-6
C13 = 13.0 / 3.0
NX, NY, NZ = 3, 16, 128
ROWS = 24


def loop(count, body):
    def step(i, carry):
        body(i)
        return carry

    lax.fori_loop(0, count, step, 0, unroll=True)


def sq(x):
    return x * x


def rcp(x):
    r = pl.reciprocal(x, approx=True)
    return r * (2.0 - x * r)


def iota(shape, dim):
    return lax.broadcasted_iota(jnp.int32, shape, dim)


def betas(w):
    n = w.shape[0] - 4
    d = w[1:] - w[:-1]
    dd = d[1:] - d[:-1]
    e = (C13 * dd) * dd + EPS
    t = dd[1:] - dd[:-1]
    left = e[:n] + sq(3.0 * d[1 : n + 1] - d[:n])
    mid = e[1 : n + 1] + sq(d[1 : n + 1] + d[2 : n + 2])
    right = e[2 : n + 2] + sq(3.0 * d[2 : n + 2] - d[3 : n + 3])
    return w[2 : n + 2], d[1 : n + 1], d[2 : n + 2], t[:n], t[1:], left, mid, right


def upwind(f, dm, dp, tm, tp, left, mid, right):
    a, b, c = sq(mid * right), sq(left * right), 3.0 * sq(left * mid)
    return 6.0 * f + dm + 2.0 * dp - (2.0 * a * tm + c * tp) * rcp(a + 6.0 * b + c)


def downwind(f, dm, dp, tm, tp, left, mid, right):
    a, b, c = sq(mid * left), sq(left * right), 3.0 * sq(mid * right)
    return 6.0 * f - dp - 2.0 * dm + (2.0 * a * tp + c * tm) * rcp(a + 6.0 * b + c)


def z_change(fp, fm):
    lane = iota(fp.shape, 1)
    first, last = lane == 0, lane == NZ - 1
    down = lambda x: pltpu.roll(x, 1, 1)
    up = lambda x: pltpu.roll(x, NZ - 1, 1)

    def parts(f):
        dp = jnp.where(last, 0.0, up(f) - f)
        dm = down(dp)
        dd = dp - dm
        e = (C13 * dd) * dd + EPS
        left, right = e + sq(3.0 * dp - dm), e + sq(3.0 * dm - dp)
        mid = e + sq(dp + dm)
        tm = dd - jnp.where(first, 0.0, down(dd))
        tp = jnp.where(last, 0.0, up(dd)) - dd
        args = (f, dm, dp, tm, tp, jnp.where(first, EPS, down(left)), mid, jnp.where(last, EPS, up(right)))
        return args, dd, left, right

    plus, dd_plus, _, right = parts(fp)
    minus, dd_minus, left, _ = parts(fm)
    rp, rm = upwind(*plus), downwind(*minus)
    f = jnp.where(first, fp, fm)
    dd = jnp.where(first, dd_plus, dd_minus)
    far = jnp.where(first, right, left)
    edge = 6.0 * f - 3.0 * EPS * EPS * dd * rcp(7.0 * sq(far) + 3.0 * EPS * EPS)
    return rp - jnp.where(first, edge, down(rp)) + jnp.where(last, edge, up(rm)) - rm


def inverse_pressure(u):
    rinv = 1.0 / u[0]
    kinetic = (u[1] * u[1] + u[2] * u[2] + u[3] * u[3]) * rinv
    return rinv, 0.4 * (u[4] - 0.5 * kinetic)


def split(u, rinv, p, direction, speed):
    normal = u[1 + direction] * rinv
    result = []
    for v in range(5):
        if v == 0:
            f = u[1 + direction]
        elif v == 4:
            f = normal * (u[4] + p)
        else:
            f = normal * u[v]
            if v == 1 + direction:
                f = f + p
        s = speed * u[v]
        result.append((f + s, f - s))
    return result


OTHER = [8, 15, 14, 13, 12, 11, 10, 9]
NEAR = [0, 1, 2, 3, 4, 5, 6, 10, 11, 12, 13, 14, 15, 16 + 1, 16 + 2, 16 + 3, 16 + 4, 16 + 5, 16 + 6]
FAR = [7, 8, 9, 16 + 7, 16 + 0]
ORDER = NEAR + FAR
PLACE = {row: place for place, row in enumerate(ORDER)}
PARTS = (slice(0, 7), slice(10, 16), slice(7, 10))


def kernel(
    n_gx, n_gy, lf_h, state_h, cell_h, frac_h, donor_h, out,
    stv, cellv, fracv, donv, fsend, frecv, isend, irecv, kq, cq, ss, pp, bs, ohs, am, maskv,
    fil, beyond, yl, yr, fx, fy, fz, fluxy, chg, ahead, lf,
    in_sem, fs_sem, fr_sem, is_sem, ir_sem, hs_sem, hr_sem, xs_sem, xr_sem, ds_sem, dr_sem, here_sem,
):
    gx, gy = lax.axis_index("gx"), lax.axis_index("gy")
    right, left, above, below = gx + 1, gx - 1, gy + 1, gy - 1
    has_left, has_right, has_below, has_above = gx > 0, gx < n_gx - 1, gy > 0, gy < n_gy - 1
    half = iota((1, 128), 1) < 64
    even = lax.rem(gx, 2) == 0
    near_left = has_left & (lax.rem(gx, 8) != 0)
    far_left = has_left & (lax.rem(gx, 8) == 0)
    far_right = has_right & (lax.rem(gx, 8) == 7)

    def partner(off):
        return lax.rem(gy + off, n_gy)

    barrier = pltpu.get_barrier_semaphore()
    for off in sorted(range(1, n_gy), key=lambda off: -min(off, n_gy - off)):
        pl.semaphore_signal(barrier, inc=1, device_id={"gy": partner(off)}, device_id_type=MESH)
    for inside, other in ((near_left, left), (has_right, right)):

        @pl.when(inside & even)
        def _():
            pl.semaphore_signal(barrier, inc=1, device_id={"gx": other}, device_id_type=MESH)

    @pl.when(far_left)
    def _():
        for off in range(n_gy):
            where = {"gx": left, "gy": partner(off)}
            pl.semaphore_signal(barrier, inc=1, device_id=where, device_id_type=MESH)

    loads = [
        pltpu.make_async_copy(src, dst, in_sem.at[i])
        for i, (src, dst) in enumerate(
            ((frac_h, fracv), (donor_h, donv), (state_h, stv.at[0]), (cell_h, cellv), (lf_h, lf))
        )
    ]
    for load in loads:
        load.start()

    def turn(x):
        return pltpu.roll(x, 64, x.ndim - 1)

    def share(tails):
        low = [jnp.where(half, a, turn(b)) for a, b in zip(tails[0::2], tails[1::2])]
        high = [jnp.where(half, turn(a), b) for a, b in zip(tails[0::2], tails[1::2])]
        return low + [tails[-1]], high + [turn(tails[-1])]

    def unshare(low, high):
        rows = []
        for a, b in zip(low, high):
            rows += [jnp.where(half, a, turn(b)), jnp.where(half, turn(a), b)]
        return rows[:-1]

    def by_distance(ref, *lead):
        rows = jnp.concatenate([ref[(*lead, pl.ds(partner(off), 1))] for off in range(16)], axis=0)
        tail = rows[:, 128:192]
        high = jnp.concatenate([tail[off : off + 1] for off in OTHER], axis=0)
        return rows[:, 0:128], jnp.concatenate([tail[0:8], high], axis=1)

    loads[0].wait()
    fsend[...] = jnp.zeros_like(fsend)
    tails = []
    for c in range(3):
        main, tail = by_distance(fracv, c)
        fsend[pl.ds(c, 16, 8), :] = main
        tails.append(tail)
    low, high = share(tails)
    for c in range(2):
        fsend[pl.ds(3 + c, 8, 8), :] = low[c]
        for t, off in enumerate(OTHER):
            fsend[off * 8 + 3 + c : off * 8 + 4 + c, :] = high[c][t : t + 1]
    beside_me = has_left.astype(jnp.int32) + jnp.where(far_right, n_gy, has_right.astype(jnp.int32))
    pl.semaphore_wait(barrier, n_gy - 1 + jnp.where(even, 0, beside_me))

    def message(send, recv, off, s_sem, r_sem):
        copy = pltpu.make_async_remote_copy(
            src_ref=send.at[pl.ds(off * 8, 8), :],
            dst_ref=recv.at[pl.ds((n_gy - off) * 8, 8), :],
            send_sem=s_sem.at[off - 1],
            recv_sem=r_sem.at[n_gy - off - 1],
            device_id={"gy": partner(off)},
            device_id_type=MESH,
        )
        return copy

    def from_source(copies):
        return {n_gy - off: copy for off, copy in copies.items()}

    offs = [off for t in (0, 7, 6, 5, 4, 3, 2, 1) for off in (OTHER[t], t) if off]
    frac_copies = {off: message(fsend, frecv, off, fs_sem, fr_sem) for off in offs}
    for copy in frac_copies.values():
        copy.start()
    frecv[0:8] = fsend[0:8]

    def beside(src, dsts, i):
        return [
            pltpu.make_async_remote_copy(
                src_ref=src,
                dst_ref=dsts[side],
                send_sem=xs_sem.at[2 * i + side],
                recv_sem=xr_sem.at[2 * i + side],
                device_id={"gx": other},
                device_id_type=MESH,
            )
            for side, other in enumerate((right, left))
        ]

    for inside, other, side in ((has_left, left, 1), (has_right, right, 0)):

        @pl.when(inside & ~even)
        def _():
            pl.semaphore_signal(here_sem.at[side], inc=1, device_id={"gx": other}, device_id_type=MESH)

    loads[3].wait()
    loads[2].wait()
    main, tail = by_distance(cellv)
    packed = jnp.concatenate([main, tail], axis=0)
    cq[0] = jnp.where(packed < 0, -4096, packed)
    loads[1].wait()
    main, tail = by_distance(donv)
    kq[...] = jnp.concatenate([main, tail], axis=0)
    flat = stv[0].reshape(240, 128)
    high = flat.astype(BF16)
    ss[:, 0:128] = high
    ss[:, 128:256] = (flat - high.astype(F32)).astype(BF16)

    def corners(r):
        donor = kq[pl.ds(r, 1), :]
        k = jnp.bitwise_and(donor, 127)
        i0 = jnp.right_shift(donor, 11)
        at = iota((128, 128), 0) - k
        here = jnp.where(at == 0, 1.0, 0.0).astype(F32)
        step = jnp.where(at == 1, 1.0, -here)
        here, step = here.astype(BF16), step.astype(BF16)
        z = jnp.concatenate(
            [jnp.concatenate([here, here], axis=0), jnp.concatenate([step, step], axis=0)], axis=1
        )
        t = jnp.dot(ss[...], z, preferred_element_type=F32)
        for c in range(2):
            tc = t[:, c * 128 : (c + 1) * 128].reshape(5, NX, NY, 128)
            x0 = jnp.where(i0 == 0, tc[:, 0], tc[:, 1])
            x1 = jnp.where(i0 == 0, tc[:, 1], tc[:, 2])
            pp[r, 2 * c] = x0
            pp[r, 2 * c + 1] = x1 - x0

    loop(ROWS, corners)

    list_copies = beside(cq.at[0], [cq.at[1], cq.at[2]], 0)
    raw_copies = beside(stv.at[0], [stv.at[1], stv.at[2]], 1)
    for copies in (list_copies, raw_copies):
        pl.when(far_right)(copies[0].start)

    def image(r, f0, f1, f2):
        donor = kq[r : r + 1, :]
        j0 = jnp.bitwise_and(jnp.right_shift(donor, 7), 15)
        at = iota((NY, 128), 0) - j0
        wy = jnp.where(at == 0, 1.0 - f1, jnp.where(at == 1, f1, 0.0))
        value = pp[r, 0] + f0 * pp[r, 1] + f2 * (pp[r, 2] + f0 * pp[r, 3])
        return jnp.sum(value * wy, axis=1)

    def row_of(ref, off, c):
        return ref[off * 8 + c : off * 8 + c + 1, :]

    sources = from_source(frac_copies)
    image_copies = {}
    direct = {
        off: pltpu.make_async_remote_copy(
            src_ref=isend.at[pl.ds(off * 8, 8), :],
            dst_ref=irecv.at[1, pl.ds((n_gy - off) % n_gy * 8, 8), :],
            send_sem=ds_sem.at[off],
            recv_sem=dr_sem.at[(n_gy - off) % n_gy],
            device_id={"gx": right, "gy": partner(off)},
            device_id_type=MESH,
        )
        for off in range(n_gy)
    }
    from_left = {(n_gy - off) % n_gy: copy for off, copy in direct.items()}
    for t in (1, 2, 3, 4, 5, 6, 7, 0):
        both = (OTHER[t], t)
        for off in both:
            if off:
                sources[off].wait_recv()
        for off in both:
            isend[off * 8 : off * 8 + 5, :] = image(off, *(row_of(frecv, off, c) for c in range(3)))
        fracs = unshare(*([row_of(frecv, off, 3 + c) for c in range(2)] for off in (t, OTHER[t])))
        value = image(16 + t, *fracs)
        low, high = share([value[v : v + 1] for v in range(5)])
        for c in range(3):
            isend[t * 8 + 5 + c : t * 8 + 6 + c, :] = low[c]
            isend[OTHER[t] * 8 + 5 + c : OTHER[t] * 8 + 6 + c, :] = high[c]
        for off in both:
            pl.when(far_right)(direct[off].start)
        for off in both:
            if off:
                image_copies[off] = message(isend, irecv.at[0], off, is_sem, ir_sem)
                pl.when(~far_right)(image_copies[off].start)
    for off in offs:
        pl.when(far_right)(image_copies[off].start)
    irecv[0, 0:8] = isend[0:8]
    by_source = from_source(image_copies)

    loads[4].wait()
    nt = (((1,), (1,)), ((), ()))

    def places(b):
        for row in range(ROWS):
            where = slice(PLACE[row] * 128, PLACE[row] * 128 + 128)
            cell = cq[b, row : row + 1, :]
            j = jnp.right_shift(cell, 7)
            column = jnp.bitwise_or(jnp.bitwise_and(jnp.right_shift(cell, 3), 128), jnp.bitwise_and(cell, 127))
            line = jnp.bitwise_or(jnp.left_shift(jnp.right_shift(cell, 11), 3), jnp.bitwise_and(j, 7))
            bs[b, :, where] = jnp.where(iota((256, 128), 0) == column, 1.0, 0.0).astype(BF16)
            i48 = iota((48, 128), 0)
            want = jnp.bitwise_or(jnp.left_shift(jnp.right_shift(i48, 4), 3), jnp.bitwise_and(i48, 7))
            ohs[b, :, where] = jnp.where(want == line, 1.0, 0.0).astype(BF16)
        count = lax.dot_general(ohs[b], bs[b], nt, preferred_element_type=F32).reshape(NX, 2, 8, 256)
        maskv[b, :, 0:8] = count[:, 0, :, 0:128]
        maskv[b, :, 8:16] = count[:, 0, :, 128:256]

    def spread(b, rows):
        for row in rows:
            where = slice(PLACE[row] * 128, PLACE[row] * 128 + 128)
            if row < 16:
                ghost = [irecv[b, row * 8 + v : row * 8 + v + 1, :] for v in range(5)]
            else:
                ends = (row - 16, OTHER[row - 16])
                low, high = ([irecv[b, a * 8 + 5 + c : a * 8 + 6 + c, :] for c in range(3)] for a in ends)
                ghost = unshare(low, high)
            lines = ohs[b, :, where].reshape(NX, 16, 128)
            for v in range(5):
                g = jnp.broadcast_to(SIGN[v] * ghost[v], (8, 128))
                hi = g.astype(BF16)
                lo = (g - hi.astype(F32)).astype(BF16)
                both = jnp.concatenate([hi, lo], axis=0)
                am[b, v * 48 : (v + 1) * 48, where] = (lines * both[None]).reshape(48, 128)

    def collect(b, rows):
        where = slice(PLACE[rows[0]] * 128, (PLACE[rows[-1]] + 1) * 128)
        return lax.dot_general(am[b, :, where], bs[b, :, where], nt, preferred_element_type=F32)

    def filled(b, total, tile):
        total = total.reshape(5, NX, 2, 8, 256)[..., tile * 128 : (tile + 1) * 128]
        rows = slice(tile * 8, tile * 8 + 8)
        return jnp.where(maskv[b, :, rows][None] > 0.5, total[:, :, 0] + total[:, :, 1], stv[b, :, :, rows])

    slices = [slice(part.start * 8, part.stop * 8) for part in PARTS]
    passed = [beside(irecv.at[0, rows], [irecv.at[1, rows], irecv.at[2, rows]], 2 + i) for i, rows in enumerate(slices)]
    side_copies = [list_copies, raw_copies] + passed

    def start(copies, to_right=has_right):
        pl.when(to_right)(copies[0].start)
        pl.when(near_left)(copies[1].start)

    def arrived(copies, side):
        pl.when((has_left, has_right)[side])(copies[side].wait_recv)

    def answered(side, expected):
        @pl.when(expected & even)
        def _():
            pl.semaphore_wait(here_sem.at[side], 1)

    answered(0, near_left)
    answered(1, has_right)
    start(list_copies, has_right & ~far_right)
    start(raw_copies, has_right & ~far_right)
    places(0)
    arrived(list_copies, 1)
    places(2)

    @pl.when(near_left)
    def _():
        list_copies[0].wait_recv()
        places(1)

    for i, part in enumerate(PARTS):
        for off in range(part.start, part.stop):
            if off:
                by_source[off].wait_recv()
        start(passed[i], has_right & ~far_right)
    spread(0, ORDER)
    total = collect(0, ORDER)
    for tile in range(2):
        fil[:, :, tile * 8 : tile * 8 + 8] = filled(0, total, tile)
    halos = {
        name: (
            pltpu.make_async_remote_copy(
                src_ref=src, dst_ref=dst, send_sem=hs_sem.at[i], recv_sem=hr_sem.at[i], device_id=where, device_id_type=MESH
            ),
            sends,
            receives,
        )
        for i, (name, src, dst, where, sends, receives) in enumerate(
            (
                ("yl", fil.at[:, :, 13:16, :], yl.at[:, :, 5:8, :], {"gy": above}, has_above, has_below),
                ("yr", fil.at[:, :, 0:3, :], yr.at[:, :, 0:3, :], {"gy": below}, has_below, has_above),
            )
        )
    }
    for copy, sends, _ in halos.values():
        pl.when(sends)(copy.start)

    u = [fil[v] for v in range(5)]
    rinv, p = inverse_pressure(u)
    for v, pair in enumerate(split(u, rinv, p, 2, lf[2])):
        for s in range(2):
            fz[s, v * NX : (v + 1) * NX] = pair[s]
    for v, pair in enumerate(split(u, rinv, p, 1, lf[1])):
        for s in range(2):
            for i in range(NX):
                fy[pl.ds((s * 32 + 8) * 16 + v * NX + i, 16, 16), :] = pair[s][i]
    for v, pair in enumerate(split(u, rinv, p, 0, lf[0])):
        for s in range(2):
            fx[s, v, 3:6] = pair[s]

    def along_z(n):
        chg[n] = z_change(fz[0, n], fz[1, n])

    loop(15, along_z)

    for copy, _, receives in halos.values():
        pl.when(receives)(copy.wait_recv)
    for edge, ref, row, base in ((~has_below, yl, 0, 0), (~has_above, yr, 15, 24)):
        u = [jnp.where(edge, fil[v, :, row : row + 1, :], ref[v]) for v in range(5)]
        rinv, p = inverse_pressure(u)
        for v, pair in enumerate(split(u, rinv, p, 1, lf[1])):
            for s in range(2):
                for i in range(NX):
                    fy[pl.ds((s * 32 + base) * 16 + v * NX + i, 8, 16), :] = pair[s][i]

    def along_y(n):
        b, h = n // 2, n % 2

        def window(s, start, count):
            return jnp.stack([fy[pl.ds(pl.multiple_of((s * 32 + start + q) * 16 + h * 8, 8), 8), :] for q in range(count)])

        flux = upwind(*betas(window(0, 5 + 3 * b, 7))) + downwind(*betas(window(1, 6 + 3 * b, 7)))
        for q in range(3):
            fluxy[pl.ds(pl.multiple_of((3 * b + q) * 16 + h * 8, 8), 8), :] = flux[q]

    loop(12, along_y)
    for n in range(15):
        chg[n] = chg[n] + (fluxy[pl.ds(16 + n, 16, 16), :] - fluxy[pl.ds(n, 16, 16), :])

    answered(0, far_left)
    for copies in side_copies:
        pl.when(far_left)(copies[1].start)
    @pl.when(far_left)
    def _():
        list_copies[0].wait_recv()
        places(1)

    def parts_arrived(side, which):
        for i in which:
            if side == 2:
                arrived(passed[i], 1)
            else:
                pl.when(near_left)(passed[i][0].wait_recv)

                @pl.when(far_left)
                def _():
                    for off in range(PARTS[i].start, PARTS[i].stop):
                        from_left[off].wait_recv()

    def ahead_x(n):
        v, h = n // 2, n % 2
        rows = pl.ds(pl.multiple_of(h * 8, 8), 8)
        ahead[0:1, v, rows] = upwind(*betas(fx[0, v, 3:8, rows]))
        ahead[1:3, v, rows] = downwind(*betas(fx[1, v, 3:9, rows]))

    for side, inside, row, base in ((2, has_right, 2, 6), (1, has_left, 0, 0)):

        @pl.when(inside)
        def _():
            parts_arrived(side, (0, 1))
            spread(side, NEAR)
            total = collect(side, NEAR)
            parts_arrived(side, (2,))
            spread(side, FAR)
            total = total + collect(side, FAR)
            arrived(raw_copies, side - 1)
            for tile in range(2):
                beyond[:, :, tile * 8 : tile * 8 + 8] = filled(side, total, tile)

        @pl.when(~inside)
        def _():
            for i in range(NX):
                beyond[:, i] = fil[:, row]

        u = [beyond[v] for v in range(5)]
        rinv, p = inverse_pressure(u)
        for v, pair in enumerate(split(u, rinv, p, 0, lf[0])):
            for s in range(2):
                fx[s, v, base : base + 3] = pair[s]
        if side == 2:
            loop(10, ahead_x)

    def along_x(n):
        v, h = n // 2, n % 2
        rows = pl.ds(pl.multiple_of(h * 8, 8), 8)
        up, down = upwind(*betas(fx[0, v, 0:7, rows])), downwind(*betas(fx[1, v, 1:7, rows]))
        flux = [up[0] + down[0], up[1] + down[1], up[2] + ahead[1, v, rows], ahead[0, v, rows] + ahead[2, v, rows]]
        flux = jnp.stack(flux)
        change = flux[1:] - flux[:-1] + chg[pl.ds(v * NX, NX), rows]
        mine = fil[v, :, rows]
        out[v, :, rows] = jnp.where(maskv[0, :, rows] > 0.5, mine, mine - (0.125 / 6.0) * change)

    loop(10, along_x)
    for copy in [*frac_copies.values(), *image_copies.values()]:
        copy.wait_send()
    for copy, sends, _ in halos.values():
        pl.when(sends)(copy.wait_send)
    for copies in side_copies:
        to_right = has_right if copies is list_copies or copies is raw_copies else has_right & ~far_right
        pl.when(to_right)(copies[0].wait_send)
        pl.when(has_left)(copies[1].wait_send)
    for copy in direct.values():
        pl.when(far_right)(copy.wait_send)


def solution(mesh):
    n_gx, n_gy = mesh.shape["gx"], mesh.shape["gy"]

    def on_device(state, lf_speed, ghost_cell, ghost_frac, donor_block):
        hbm = pl.BlockSpec(memory_space=pltpu.HBM)
        vmem = pltpu.VMEM
        dma = pltpu.SemaphoreType.DMA
        brick = (5, NX, NY, NZ)
        return pl.pallas_call(
            functools.partial(kernel, n_gx, n_gy),
            out_shape=jax.ShapeDtypeStruct(brick, F32),
            in_specs=[hbm] * 5,
            out_specs=pl.BlockSpec(memory_space=pltpu.VMEM),
            scratch_shapes=[
                vmem((3,) + brick, F32),
                vmem((16, 192), jnp.int32),
                vmem((3, 16, 192), F32),
                vmem((16, 192), jnp.int32),
                vmem((128, 128), F32),
                vmem((128, 128), F32),
                vmem((128, 128), F32),
                vmem((3, 128, 128), F32),
                vmem((ROWS, 128), jnp.int32),
                vmem((3, ROWS, 128), jnp.int32),
                vmem((240, 256), BF16),
                vmem((ROWS, 4, 5, NY, 128), F32),
                vmem((3, 256, ROWS * 128), BF16),
                vmem((3, 48, ROWS * 128), BF16),
                vmem((3, 240, ROWS * 128), BF16),
                vmem((3, NX, NY, NZ), F32),
                vmem(brick, F32),
                vmem(brick, F32),
                vmem((5, NX, 8, NZ), F32),
                vmem((5, NX, 8, NZ), F32),
                vmem((2, 5, 9, NY, NZ), F32),
                vmem((2 * 32 * 16, NZ), F32),
                vmem((2, 15, NY, NZ), F32),
                vmem((18 * 16, NZ), F32),
                vmem((15, NY, NZ), F32),
                vmem((3, 5, NY, NZ), F32),
                pltpu.SMEM((3,), F32),
                dma((5,)),
                dma((n_gy - 1,)),
                dma((n_gy - 1,)),
                dma((n_gy - 1,)),
                dma((n_gy - 1,)),
                dma((2,)),
                dma((2,)),
                dma((10,)),
                dma((10,)),
                dma((n_gy,)),
                dma((n_gy,)),
                pltpu.SemaphoreType.REGULAR((2,)),
            ],
            compiler_params=pltpu.CompilerParams(
                collective_id=0, has_side_effects=True, vmem_limit_bytes=40 * 1024 * 1024
            ),
        )(
            *(
                pltpu.with_memory_space_constraint(x, pltpu.HBM)
                for x in (
                    lf_speed,
                    state,
                    ghost_cell.reshape(ghost_cell.shape[2:]),
                    ghost_frac.reshape((3,) + ghost_frac.shape[3:]),
                    donor_block.reshape(donor_block.shape[2:]),
                )
            )
        )

    return jax.shard_map(
        on_device,
        mesh=mesh,
        in_specs=(
            P(None, "gx", "gy", None),
            P(),
            P("gx", "gy", None, None),
            P(None, "gx", "gy", None, None),
            P("gx", "gy", None, None),
        ),
        out_specs=P(None, "gx", "gy", None),
        check_vma=False,
    )
```

```python
import functools

import jax
import jax.numpy as jnp
from jax import lax
from jax.experimental import pallas as pl
from jax.experimental.pallas import tpu as pltpu
from jax.sharding import PartitionSpec as P

MESH = pl.DeviceIdType.MESH
F32 = jnp.float32
BF16 = jnp.bfloat16
SIGN = (1.0, -1.0, -1.0, -1.0, 1.0)
EPS = 16.0e-6
C13 = 13.0 / 3.0
NX, NY, NZ = 3, 16, 128
ROWS = 24


def loop(count, body):
    def step(i, carry):
        body(i)
        return carry

    lax.fori_loop(0, count, step, 0, unroll=True)


def sq(x):
    return x * x


def rcp(x):
    r = pl.reciprocal(x, approx=True)
    return r * (2.0 - x * r)


def iota(shape, dim):
    return lax.broadcasted_iota(jnp.int32, shape, dim)


def betas(w):
    n = w.shape[0] - 4
    d = w[1:] - w[:-1]
    dd = d[1:] - d[:-1]
    e = (C13 * dd) * dd + EPS
    t = dd[1:] - dd[:-1]
    left = e[:n] + sq(3.0 * d[1 : n + 1] - d[:n])
    mid = e[1 : n + 1] + sq(d[1 : n + 1] + d[2 : n + 2])
    right = e[2 : n + 2] + sq(3.0 * d[2 : n + 2] - d[3 : n + 3])
    return w[2 : n + 2], d[1 : n + 1], d[2 : n + 2], t[:n], t[1:], left, mid, right


def upwind(f, dm, dp, tm, tp, left, mid, right):
    a, b, c = sq(mid * right), sq(left * right), 3.0 * sq(left * mid)
    return 6.0 * f + dm + 2.0 * dp - (2.0 * a * tm + c * tp) * rcp(a + 6.0 * b + c)


def downwind(f, dm, dp, tm, tp, left, mid, right):
    a, b, c = sq(mid * left), sq(left * right), 3.0 * sq(mid * right)
    return 6.0 * f - dp - 2.0 * dm + (2.0 * a * tp + c * tm) * rcp(a + 6.0 * b + c)


def z_change(fp, fm):
    lane = iota(fp.shape, 1)
    first, last = lane == 0, lane == NZ - 1
    down = lambda x: pltpu.roll(x, 1, 1)
    up = lambda x: pltpu.roll(x, NZ - 1, 1)

    def parts(f):
        dp = jnp.where(last, 0.0, up(f) - f)
        dm = down(dp)
        dd = dp - dm
        e = (C13 * dd) * dd + EPS
        left, right = e + sq(3.0 * dp - dm), e + sq(3.0 * dm - dp)
        mid = e + sq(dp + dm)
        tm = dd - jnp.where(first, 0.0, down(dd))
        tp = jnp.where(last, 0.0, up(dd)) - dd
        args = (f, dm, dp, tm, tp, jnp.where(first, EPS, down(left)), mid, jnp.where(last, EPS, up(right)))
        return args, dd, left, right

    plus, dd_plus, _, right = parts(fp)
    minus, dd_minus, left, _ = parts(fm)
    rp, rm = upwind(*plus), downwind(*minus)
    f = jnp.where(first, fp, fm)
    dd = jnp.where(first, dd_plus, dd_minus)
    far = jnp.where(first, right, left)
    edge = 6.0 * f - 3.0 * EPS * EPS * dd * rcp(7.0 * sq(far) + 3.0 * EPS * EPS)
    return rp - jnp.where(first, edge, down(rp)) + jnp.where(last, edge, up(rm)) - rm


def inverse_pressure(u):
    rinv = 1.0 / u[0]
    kinetic = (u[1] * u[1] + u[2] * u[2] + u[3] * u[3]) * rinv
    return rinv, 0.4 * (u[4] - 0.5 * kinetic)


def split(u, rinv, p, direction, speed):
    normal = u[1 + direction] * rinv
    result = []
    for v in range(5):
        if v == 0:
            f = u[1 + direction]
        elif v == 4:
            f = normal * (u[4] + p)
        else:
            f = normal * u[v]
            if v == 1 + direction:
                f = f + p
        s = speed * u[v]
        result.append((f + s, f - s))
    return result


OTHER = [8, 15, 14, 13, 12, 11, 10, 9]
NEAR = [0, 1, 2, 3, 4, 5, 6, 10, 11, 12, 13, 14, 15, 16 + 1, 16 + 2, 16 + 3, 16 + 4, 16 + 5, 16 + 6]
FAR = [7, 8, 9, 16 + 7, 16 + 0]
ORDER = NEAR + FAR
PLACE = {row: place for place, row in enumerate(ORDER)}
PARTS = (slice(0, 7), slice(10, 16), slice(7, 10))


def kernel(
    n_gx, n_gy, lf_h, state_h, cell_h, frac_h, donor_h, out,
    stv, cellv, fracv, donv, fsend, frecv, isend, irecv, kq, cq, ss, pp, bs, ohs, am, maskv,
    fil, beyond, yl, yr, fx, fy, fz, fluxy, chg, ahead, lf,
    in_sem, fs_sem, fr_sem, is_sem, ir_sem, hs_sem, hr_sem, xs_sem, xr_sem, ds_sem, dr_sem, here_sem,
):
    gx, gy = lax.axis_index("gx"), lax.axis_index("gy")
    right, left, above, below = gx + 1, gx - 1, gy + 1, gy - 1
    has_left, has_right, has_below, has_above = gx > 0, gx < n_gx - 1, gy > 0, gy < n_gy - 1
    half = iota((1, 128), 1) < 64
    even = lax.rem(gx, 2) == 0
    near_left = has_left & (lax.rem(gx, 8) != 0)
    far_left = has_left & (lax.rem(gx, 8) == 0)
    far_right = has_right & (lax.rem(gx, 8) == 7)

    def partner(off):
        return lax.rem(gy + off, n_gy)

    barrier = pltpu.get_barrier_semaphore()
    for off in sorted(range(1, n_gy), key=lambda off: -min(off, n_gy - off)):
        pl.semaphore_signal(barrier, inc=1, device_id={"gy": partner(off)}, device_id_type=MESH)
    for inside, other in ((near_left, left), (has_right, right)):

        @pl.when(inside & even)
        def _():
            pl.semaphore_signal(barrier, inc=1, device_id={"gx": other}, device_id_type=MESH)

    @pl.when(far_left)
    def _():
        for off in range(n_gy):
            where = {"gx": left, "gy": partner(off)}
            pl.semaphore_signal(barrier, inc=1, device_id=where, device_id_type=MESH)

    loads = [
        pltpu.make_async_copy(src, dst, in_sem.at[i])
        for i, (src, dst) in enumerate(
            ((frac_h, fracv), (donor_h, donv), (state_h, stv.at[0]), (cell_h, cellv), (lf_h, lf))
        )
    ]
    for load in loads:
        load.start()

    def turn(x):
        return pltpu.roll(x, 64, x.ndim - 1)

    def share(tails):
        low = [jnp.where(half, a, turn(b)) for a, b in zip(tails[0::2], tails[1::2])]
        high = [jnp.where(half, turn(a), b) for a, b in zip(tails[0::2], tails[1::2])]
        return low + [tails[-1]], high + [turn(tails[-1])]

    def unshare(low, high):
        rows = []
        for a, b in zip(low, high):
            rows += [jnp.where(half, a, turn(b)), jnp.where(half, turn(a), b)]
        return rows[:-1]

    def by_distance(ref, *lead):
        rows = jnp.concatenate([ref[(*lead, pl.ds(partner(off), 1))] for off in range(16)], axis=0)
        tail = rows[:, 128:192]
        high = jnp.concatenate([tail[off : off + 1] for off in OTHER], axis=0)
        return rows[:, 0:128], jnp.concatenate([tail[0:8], high], axis=1)

    loads[0].wait()
    fsend[...] = jnp.zeros_like(fsend)
    tails = []
    for c in range(3):
        main, tail = by_distance(fracv, c)
        fsend[pl.ds(c, 16, 8), :] = main
        tails.append(tail)
    low, high = share(tails)
    for c in range(2):
        fsend[pl.ds(3 + c, 8, 8), :] = low[c]
        for t, off in enumerate(OTHER):
            fsend[off * 8 + 3 + c : off * 8 + 4 + c, :] = high[c][t : t + 1]
    beside_me = has_left.astype(jnp.int32) + jnp.where(far_right, n_gy, has_right.astype(jnp.int32))
    pl.semaphore_wait(barrier, n_gy - 1 + jnp.where(even, 0, beside_me))

    def message(send, recv, off, s_sem, r_sem):
        copy = pltpu.make_async_remote_copy(
            src_ref=send.at[pl.ds(off * 8, 8), :],
            dst_ref=recv.at[pl.ds((n_gy - off) * 8, 8), :],
            send_sem=s_sem.at[off - 1],
            recv_sem=r_sem.at[n_gy - off - 1],
            device_id={"gy": partner(off)},
            device_id_type=MESH,
        )
        return copy

    def from_source(copies):
        return {n_gy - off: copy for off, copy in copies.items()}

    offs = [off for t in (0, 7, 6, 5, 4, 3, 2, 1) for off in (OTHER[t], t) if off]
    frac_copies = {off: message(fsend, frecv, off, fs_sem, fr_sem) for off in offs}
    for copy in frac_copies.values():
        copy.start()
    frecv[0:8] = fsend[0:8]

    def beside(src, dsts, i):
        return [
            pltpu.make_async_remote_copy(
                src_ref=src,
                dst_ref=dsts[side],
                send_sem=xs_sem.at[2 * i + side],
                recv_sem=xr_sem.at[2 * i + side],
                device_id={"gx": other},
                device_id_type=MESH,
            )
            for side, other in enumerate((right, left))
        ]

    for inside, other, side in ((has_left, left, 1), (has_right, right, 0)):

        @pl.when(inside & ~even)
        def _():
            pl.semaphore_signal(here_sem.at[side], inc=1, device_id={"gx": other}, device_id_type=MESH)

    loads[3].wait()
    loads[2].wait()
    main, tail = by_distance(cellv)
    packed = jnp.concatenate([main, tail], axis=0)
    cq[0] = jnp.where(packed < 0, -4096, packed)
    loads[1].wait()
    main, tail = by_distance(donv)
    kq[...] = jnp.concatenate([main, tail], axis=0)
    flat = stv[0].reshape(240, 128)
    high = flat.astype(BF16)
    ss[:, 0:128] = high
    ss[:, 128:256] = (flat - high.astype(F32)).astype(BF16)

    def corners(r):
        donor = kq[pl.ds(r, 1), :]
        k = jnp.bitwise_and(donor, 127)
        i0 = jnp.right_shift(donor, 11)
        at = iota((128, 128), 0) - k
        here = jnp.where(at == 0, 1.0, 0.0).astype(F32)
        step = jnp.where(at == 1, 1.0, -here)
        here, step = here.astype(BF16), step.astype(BF16)
        z = jnp.concatenate(
            [jnp.concatenate([here, here], axis=0), jnp.concatenate([step, step], axis=0)], axis=1
        )
        t = jnp.dot(ss[...], z, preferred_element_type=F32)
        for c in range(2):
            tc = t[:, c * 128 : (c + 1) * 128].reshape(5, NX, NY, 128)
            x0 = jnp.where(i0 == 0, tc[:, 0], tc[:, 1])
            x1 = jnp.where(i0 == 0, tc[:, 1], tc[:, 2])
            pp[r, 2 * c] = x0
            pp[r, 2 * c + 1] = x1 - x0

    loop(ROWS, corners)

    list_copies = beside(cq.at[0], [cq.at[1], cq.at[2]], 0)
    raw_copies = beside(stv.at[0], [stv.at[1], stv.at[2]], 1)
    for copies in (list_copies, raw_copies):
        pl.when(far_right)(copies[0].start)

    def image(r, f0, f1, f2):
        donor = kq[r : r + 1, :]
        j0 = jnp.bitwise_and(jnp.right_shift(donor, 7), 15)
        at = iota((NY, 128), 0) - j0
        wy = jnp.where(at == 0, 1.0 - f1, jnp.where(at == 1, f1, 0.0))
        value = pp[r, 0] + f0 * pp[r, 1] + f2 * (pp[r, 2] + f0 * pp[r, 3])
        return jnp.sum(value * wy, axis=1)

    def row_of(ref, off, c):
        return ref[off * 8 + c : off * 8 + c + 1, :]

    sources = from_source(frac_copies)
    image_copies = {}
    direct = {
        off: pltpu.make_async_remote_copy(
            src_ref=isend.at[pl.ds(off * 8, 8), :],
            dst_ref=irecv.at[1, pl.ds((n_gy - off) % n_gy * 8, 8), :],
            send_sem=ds_sem.at[off],
            recv_sem=dr_sem.at[(n_gy - off) % n_gy],
            device_id={"gx": right, "gy": partner(off)},
            device_id_type=MESH,
        )
        for off in range(n_gy)
    }
    from_left = {(n_gy - off) % n_gy: copy for off, copy in direct.items()}
    for t in (1, 2, 3, 4, 5, 6, 7, 0):
        both = (OTHER[t], t)
        for off in both:
            if off:
                sources[off].wait_recv()
        for off in both:
            isend[off * 8 : off * 8 + 5, :] = image(off, *(row_of(frecv, off, c) for c in range(3)))
        fracs = unshare(*([row_of(frecv, off, 3 + c) for c in range(2)] for off in (t, OTHER[t])))
        value = image(16 + t, *fracs)
        low, high = share([value[v : v + 1] for v in range(5)])
        for c in range(3):
            isend[t * 8 + 5 + c : t * 8 + 6 + c, :] = low[c]
            isend[OTHER[t] * 8 + 5 + c : OTHER[t] * 8 + 6 + c, :] = high[c]
        for off in both:
            pl.when(far_right)(direct[off].start)
        for off in both:
            if off:
                image_copies[off] = message(isend, irecv.at[0], off, is_sem, ir_sem)
                pl.when(~far_right)(image_copies[off].start)
    for off in offs:
        pl.when(far_right)(image_copies[off].start)
    irecv[0, 0:8] = isend[0:8]
    by_source = from_source(image_copies)

    loads[4].wait()
    nt = (((1,), (1,)), ((), ()))

    def places(b):
        for row in range(ROWS):
            where = slice(PLACE[row] * 128, PLACE[row] * 128 + 128)
            cell = cq[b, row : row + 1, :]
            j = jnp.right_shift(cell, 7)
            column = jnp.bitwise_or(jnp.bitwise_and(jnp.right_shift(cell, 3), 128), jnp.bitwise_and(cell, 127))
            line = jnp.bitwise_or(jnp.left_shift(jnp.right_shift(cell, 11), 3), jnp.bitwise_and(j, 7))
            bs[b, :, where] = jnp.where(iota((256, 128), 0) == column, 1.0, 0.0).astype(BF16)
            i48 = iota((48, 128), 0)
            want = jnp.bitwise_or(jnp.left_shift(jnp.right_shift(i48, 4), 3), jnp.bitwise_and(i48, 7))
            ohs[b, :, where] = jnp.where(want == line, 1.0, 0.0).astype(BF16)
        count = lax.dot_general(ohs[b], bs[b], nt, preferred_element_type=F32).reshape(NX, 2, 8, 256)
        maskv[b, :, 0:8] = count[:, 0, :, 0:128]
        maskv[b, :, 8:16] = count[:, 0, :, 128:256]

    def spread(b, rows):
        for row in rows:
            where = slice(PLACE[row] * 128, PLACE[row] * 128 + 128)
            if row < 16:
                ghost = [irecv[b, row * 8 + v : row * 8 + v + 1, :] for v in range(5)]
            else:
                ends = (row - 16, OTHER[row - 16])
                low, high = ([irecv[b, a * 8 + 5 + c : a * 8 + 6 + c, :] for c in range(3)] for a in ends)
                ghost = unshare(low, high)
            lines = ohs[b, :, where].reshape(NX, 16, 128)
            for v in range(5):
                g = jnp.broadcast_to(SIGN[v] * ghost[v], (8, 128))
                hi = g.astype(BF16)
                lo = (g - hi.astype(F32)).astype(BF16)
                both = jnp.concatenate([hi, lo], axis=0)
                am[b, v * 48 : (v + 1) * 48, where] = (lines * both[None]).reshape(48, 128)

    def collect(b, rows):
        where = slice(PLACE[rows[0]] * 128, (PLACE[rows[-1]] + 1) * 128)
        return lax.dot_general(am[b, :, where], bs[b, :, where], nt, preferred_element_type=F32)

    def filled(b, total, tile):
        total = total.reshape(5, NX, 2, 8, 256)[..., tile * 128 : (tile + 1) * 128]
        rows = slice(tile * 8, tile * 8 + 8)
        return jnp.where(maskv[b, :, rows][None] > 0.5, total[:, :, 0] + total[:, :, 1], stv[b, :, :, rows])

    slices = [slice(part.start * 8, part.stop * 8) for part in PARTS]
    passed = [beside(irecv.at[0, rows], [irecv.at[1, rows], irecv.at[2, rows]], 2 + i) for i, rows in enumerate(slices)]
    side_copies = [list_copies, raw_copies] + passed

    def start(copies, to_right=has_right):
        pl.when(to_right)(copies[0].start)
        pl.when(near_left)(copies[1].start)

    def arrived(copies, side):
        pl.when((has_left, has_right)[side])(copies[side].wait_recv)

    def answered(side, expected):
        @pl.when(expected & even)
        def _():
            pl.semaphore_wait(here_sem.at[side], 1)

    answered(0, near_left)
    answered(1, has_right)
    start(list_copies, has_right & ~far_right)
    start(raw_copies, has_right & ~far_right)
    places(0)
    arrived(list_copies, 1)
    places(2)

    @pl.when(near_left)
    def _():
        list_copies[0].wait_recv()
        places(1)

    for i, part in enumerate(PARTS):
        for off in range(part.start, part.stop):
            if off:
                by_source[off].wait_recv()
        start(passed[i], has_right & ~far_right)
    spread(0, ORDER)
    total = collect(0, ORDER)
    for tile in range(2):
        fil[:, :, tile * 8 : tile * 8 + 8] = filled(0, total, tile)
    halos = {
        name: (
            pltpu.make_async_remote_copy(
                src_ref=src, dst_ref=dst, send_sem=hs_sem.at[i], recv_sem=hr_sem.at[i], device_id=where, device_id_type=MESH
            ),
            sends,
            receives,
        )
        for i, (name, src, dst, where, sends, receives) in enumerate(
            (
                ("yl", fil.at[:, :, 13:16, :], yl.at[:, :, 5:8, :], {"gy": above}, has_above, has_below),
                ("yr", fil.at[:, :, 0:3, :], yr.at[:, :, 0:3, :], {"gy": below}, has_below, has_above),
            )
        )
    }
    for copy, sends, _ in halos.values():
        pl.when(sends)(copy.start)

    u = [fil[v] for v in range(5)]
    rinv, p = inverse_pressure(u)
    for v, pair in enumerate(split(u, rinv, p, 2, lf[2])):
        for s in range(2):
            fz[s, v * NX : (v + 1) * NX] = pair[s]
    for v, pair in enumerate(split(u, rinv, p, 1, lf[1])):
        for s in range(2):
            for i in range(NX):
                fy[pl.ds((s * 32 + 8) * 16 + v * NX + i, 16, 16), :] = pair[s][i]
    for v, pair in enumerate(split(u, rinv, p, 0, lf[0])):
        for s in range(2):
            fx[s, v, 3:6] = pair[s]

    def along_z(n):
        chg[n] = z_change(fz[0, n], fz[1, n])

    loop(15, along_z)

    for copy, _, receives in halos.values():
        pl.when(receives)(copy.wait_recv)
    for edge, ref, row, base in ((~has_below, yl, 0, 0), (~has_above, yr, 15, 24)):
        u = [jnp.where(edge, fil[v, :, row : row + 1, :], ref[v]) for v in range(5)]
        rinv, p = inverse_pressure(u)
        for v, pair in enumerate(split(u, rinv, p, 1, lf[1])):
            for s in range(2):
                for i in range(NX):
                    fy[pl.ds((s * 32 + base) * 16 + v * NX + i, 8, 16), :] = pair[s][i]

    def along_y(n):
        b, h = n // 2, n % 2

        def window(s, start, count):
            return jnp.stack([fy[pl.ds(pl.multiple_of((s * 32 + start + q) * 16 + h * 8, 8), 8), :] for q in range(count)])

        flux = upwind(*betas(window(0, 5 + 3 * b, 7))) + downwind(*betas(window(1, 6 + 3 * b, 7)))
        for q in range(3):
            fluxy[pl.ds(pl.multiple_of((3 * b + q) * 16 + h * 8, 8), 8), :] = flux[q]

    loop(12, along_y)
    for n in range(15):
        chg[n] = chg[n] + (fluxy[pl.ds(16 + n, 16, 16), :] - fluxy[pl.ds(n, 16, 16), :])

    answered(0, far_left)
    for copies in side_copies:
        pl.when(far_left)(copies[1].start)
    @pl.when(far_left)
    def _():
        list_copies[0].wait_recv()
        places(1)

    def parts_arrived(side, which):
        for i in which:
            if side == 2:
                arrived(passed[i], 1)
            else:
                pl.when(near_left)(passed[i][0].wait_recv)

                @pl.when(far_left)
                def _():
                    for off in range(PARTS[i].start, PARTS[i].stop):
                        from_left[off].wait_recv()

    def sent():
        for copy in [*frac_copies.values(), *image_copies.values()]:
            copy.wait_send()
        for copy, sends, _ in halos.values():
            pl.when(sends)(copy.wait_send)
        for copies in side_copies:
            to_right = has_right if copies is list_copies or copies is raw_copies else has_right & ~far_right
            pl.when(to_right)(copies[0].wait_send)
            pl.when(has_left)(copies[1].wait_send)
        for copy in direct.values():
            pl.when(far_right)(copy.wait_send)

    def ahead_x(n):
        v, h = n // 2, n % 2
        rows = pl.ds(pl.multiple_of(h * 8, 8), 8)
        ahead[0:1, v, rows] = upwind(*betas(fx[0, v, 3:8, rows]))
        ahead[1:3, v, rows] = downwind(*betas(fx[1, v, 3:9, rows]))

    for side, inside, row, base in ((2, has_right, 2, 6), (1, has_left, 0, 0)):

        @pl.when(inside)
        def _():
            parts_arrived(side, (0, 1))
            spread(side, NEAR)
            total = collect(side, NEAR)
            parts_arrived(side, (2,))
            spread(side, FAR)
            total = total + collect(side, FAR)
            arrived(raw_copies, side - 1)
            for tile in range(2):
                beyond[:, :, tile * 8 : tile * 8 + 8] = filled(side, total, tile)

        @pl.when(~inside)
        def _():
            for i in range(NX):
                beyond[:, i] = fil[:, row]

        u = [beyond[v] for v in range(5)]
        rinv, p = inverse_pressure(u)
        for v, pair in enumerate(split(u, rinv, p, 0, lf[0])):
            for s in range(2):
                fx[s, v, base : base + 3] = pair[s]
        if side == 2:
            loop(10, ahead_x)
            sent()

    def along_x(n):
        v, h = n // 2, n % 2
        rows = pl.ds(pl.multiple_of(h * 8, 8), 8)
        up, down = upwind(*betas(fx[0, v, 0:7, rows])), downwind(*betas(fx[1, v, 1:7, rows]))
        flux = [up[0] + down[0], up[1] + down[1], up[2] + ahead[1, v, rows], ahead[0, v, rows] + ahead[2, v, rows]]
        flux = jnp.stack(flux)
        change = flux[1:] - flux[:-1] + chg[pl.ds(v * NX, NX), rows]
        mine = fil[v, :, rows]
        out[v, :, rows] = jnp.where(maskv[0, :, rows] > 0.5, mine, mine - (0.125 / 6.0) * change)

    loop(10, along_x)


def solution(mesh):
    n_gx, n_gy = mesh.shape["gx"], mesh.shape["gy"]

    def on_device(state, lf_speed, ghost_cell, ghost_frac, donor_block):
        hbm = pl.BlockSpec(memory_space=pltpu.HBM)
        vmem = pltpu.VMEM
        dma = pltpu.SemaphoreType.DMA
        brick = (5, NX, NY, NZ)
        return pl.pallas_call(
            functools.partial(kernel, n_gx, n_gy),
            out_shape=jax.ShapeDtypeStruct(brick, F32),
            in_specs=[hbm] * 5,
            out_specs=pl.BlockSpec(memory_space=pltpu.VMEM),
            scratch_shapes=[
                vmem((3,) + brick, F32),
                vmem((16, 192), jnp.int32),
                vmem((3, 16, 192), F32),
                vmem((16, 192), jnp.int32),
                vmem((128, 128), F32),
                vmem((128, 128), F32),
                vmem((128, 128), F32),
                vmem((3, 128, 128), F32),
                vmem((ROWS, 128), jnp.int32),
                vmem((3, ROWS, 128), jnp.int32),
                vmem((240, 256), BF16),
                vmem((ROWS, 4, 5, NY, 128), F32),
                vmem((3, 256, ROWS * 128), BF16),
                vmem((3, 48, ROWS * 128), BF16),
                vmem((3, 240, ROWS * 128), BF16),
                vmem((3, NX, NY, NZ), F32),
                vmem(brick, F32),
                vmem(brick, F32),
                vmem((5, NX, 8, NZ), F32),
                vmem((5, NX, 8, NZ), F32),
                vmem((2, 5, 9, NY, NZ), F32),
                vmem((2 * 32 * 16, NZ), F32),
                vmem((2, 15, NY, NZ), F32),
                vmem((18 * 16, NZ), F32),
                vmem((15, NY, NZ), F32),
                vmem((3, 5, NY, NZ), F32),
                pltpu.SMEM((3,), F32),
                dma((5,)),
                dma((n_gy - 1,)),
                dma((n_gy - 1,)),
                dma((n_gy - 1,)),
                dma((n_gy - 1,)),
                dma((2,)),
                dma((2,)),
                dma((10,)),
                dma((10,)),
                dma((n_gy,)),
                dma((n_gy,)),
                pltpu.SemaphoreType.REGULAR((2,)),
            ],
            compiler_params=pltpu.CompilerParams(
                collective_id=0, has_side_effects=True, vmem_limit_bytes=40 * 1024 * 1024
            ),
        )(
            *(
                pltpu.with_memory_space_constraint(x, pltpu.HBM)
                for x in (
                    lf_speed,
                    state,
                    ghost_cell.reshape(ghost_cell.shape[2:]),
                    ghost_frac.reshape((3,) + ghost_frac.shape[3:]),
                    donor_block.reshape(donor_block.shape[2:]),
                )
            )
        )

    return jax.shard_map(
        on_device,
        mesh=mesh,
        in_specs=(
            P(None, "gx", "gy", None),
            P(),
            P("gx", "gy", None, None),
            P(None, "gx", "gy", None, None),
            P("gx", "gy", None, None),
        ),
        out_specs=P(None, "gx", "gy", None),
        check_vma=False,
    )
```
